128 devices in a mesh: lon: 16 (over x_hi, z, core), lat: 8 (over x_lo, y).
Axes of the slice: x: 4 (x_hi: 2, x_lo: 2; x = x_hi * 2 + x_lo), y: 4, z: 4, core: 2. Of those that a mesh axis runs over, the one named last changes fastest.
Arguments:
- state: bfloat16 [16, 8, 64, 512, 128], P('lon', 'lat'), may hold values from -6 to 6
- conv_w: bfloat16 [3, 8, 16, 16], replicated, may hold values from -0.875 to 0.875
- readout: float32 [128, 8], replicated, may hold values from -0.5 to 0.5
- kernel: float32 [256, 64, 8], replicated, may hold values from -0.25 to 0.25
- cross_col: int32 [16, 8, 8, 256], P('lon', 'lat'), may hold values from 0 to 511
- seg_count: int32 [16, 8, 256], P('lon', 'lat'), may hold values from 1 to 8
- seg_len: float32 [16, 8, 8, 256], P('lon', 'lat'), may hold values from 0.25 to 1
- observed: float32 [16, 8, 256, 256], P('lon', 'lat'), may hold values from -8 to 8
- obs_err: float32 [16, 8, 256, 256], P('lon', 'lat'), may hold values from 0.5 to 2
Outputs:
- grad_state: bfloat16 [16, 8, 64, 512, 128], P('lon', 'lat')
- bending: float32 [16, 8, 256, 256], P('lon', 'lat')
- grad_conv: float32 [3, 8, 16, 16], replicated
The draws below stay inside these ranges and needn't reach their ends.
Inputs may be any that keep to these rules, and one draw needn't show every extreme that they name: `cross_col`: a column of the crossed tile.
All inputs are finite; a program needn't handle non-finite values.
Results may differ from the reference program's by a relative error of at most 0.0037.
The reference program's roundings to bfloat16 on the way (of `wide` and `dact`) count: a program that leaves them out, or rounds other values in their place, can miss the bound.
Values sent between devices are 32-bit elements; how exact they have to be, the bound alone decides.
A program may use at most 192 MiB of HBM per device.

```python
import math
import jax
import jax.numpy as jnp
from jax import lax

LEV = 64
COLS = 512
RAYS_DEV = 256
GROUPS = 8
CG = 16
KS = 3
NQ = 8
IMP = 256
CH = 128
LQ = 512
SPAN = 8
LON_T = 16
LAT_T = 8


def with_ends(entries, own_key, smallest, top_value):
    longest = entries.shape.index(max(entries.shape))
    spots = []
    for shift in (0, 1):
        where = [jax.random.randint(jax.random.fold_in(own_key, axis), (), 0, length) for axis, length in enumerate(entries.shape)]
        where[longest] = (where[longest] + shift) % entries.shape[longest]
        spots.append(tuple(where))
    return entries.at[spots[0]].set(smallest).at[spots[1]].set(top_value)


def block_levels(stream_key, shape, split, least, high):
    def one(dim, blocks):
        steps = jax.random.uniform(jax.random.fold_in(jax.random.fold_in(stream_key, 6), dim), (blocks,), jnp.float32, least / len(split), high / len(split))
        return jnp.repeat(jnp.exp(steps), shape[dim] // blocks).reshape((-1,) + (1,) * (len(shape) - dim - 1))

    loudness = one(*split[0])
    for cut in split[1:]:
        loudness = loudness * one(*cut)
    return loudness


def normal_values(own_key, extent, deviation, most, split=(), kind=jnp.bfloat16):
    values = jax.random.normal(own_key, extent, jnp.float32) * deviation
    if len(split) > 0:
        values = block_levels(own_key, extent, split, -0.22, 0.18) * values
    return jnp.clip(values, min=-most, max=most).astype(kind)


def setup_inputs(seed: int = 0) -> dict:
    streams_of = jax.random.split(jax.random.key(seed), 10)
    state = normal_values(streams_of[0], (LON_T, LAT_T, LEV, COLS, CH), 1.0, 6.0, ((0, 16), (1, 8)))
    conv_w = normal_values(streams_of[1], (KS, GROUPS, CG, CG), (KS * CG) ** -0.5, 0.875)
    readout = normal_values(streams_of[2], (CH, NQ), CH ** -0.5, 0.5, (), jnp.float32)
    kernel = normal_values(streams_of[3], (IMP, LEV, NQ), (LEV * NQ) ** -0.5, 0.25, (), jnp.float32)
    cross_col = with_ends(jax.random.randint(streams_of[4], (LON_T, LAT_T, SPAN, RAYS_DEV), 0, COLS), jax.random.fold_in(streams_of[4], 1), 0, COLS - 1).astype(jnp.int32)
    seg_count = with_ends(jax.random.randint(streams_of[5], (LON_T, LAT_T, RAYS_DEV), 1, SPAN + 1), jax.random.fold_in(streams_of[5], 1), 1, SPAN).astype(jnp.int32)
    seg_len = jnp.clip(jnp.exp(math.log(1.0) - 1.3862944 * jax.random.uniform(streams_of[6], (LON_T, LAT_T, SPAN, RAYS_DEV), jnp.float32) ** block_levels(streams_of[6], (LON_T, LAT_T, SPAN, RAYS_DEV), ((0, 16), (1, 8)), -0.2, 0.2)), 0.25, 1.0)
    observed = normal_values(streams_of[7], (LON_T, LAT_T, RAYS_DEV, IMP), 2.0, 8.0, ((0, 16), (1, 8)), jnp.float32)
    obs_err = jnp.clip(jnp.exp(math.log(2.0) - 1.3862944 * jax.random.uniform(streams_of[8], (LON_T, LAT_T, RAYS_DEV, IMP), jnp.float32) ** block_levels(streams_of[8], (LON_T, LAT_T, RAYS_DEV, IMP), ((0, 16), (1, 8)), -0.2, 0.2)), 0.5, 2.0)
    return {"state": state, "conv_w": conv_w, "readout": readout, "kernel": kernel, "cross_col": cross_col, "seg_count": seg_count, "seg_len": seg_len, "observed": observed, "obs_err": obs_err}


def block_weights(conv_w):
    taps, groups, width, _ = conv_w.shape
    eye = jnp.eye(groups, dtype=jnp.float32)
    full = conv_w.astype(jnp.float32)[:, :, :, None, :] * eye[None, :, None, :, None]
    return full.reshape(taps, groups * width, groups * width)


def conv_act(column, wide):
    levels = column.shape[0]
    padded = jnp.pad(column.astype(jnp.float32), ((1, 1), (0, 0), (0, 0)))
    act = jnp.zeros(column.shape, jnp.float32)
    for tap in range(wide.shape[0]):
        act = act + jnp.einsum('lci,ij->lcj', padded[tap:tap + levels], wide[tap], precision=lax.Precision.HIGHEST)
    return act


def reference(state, conv_w, readout, kernel, cross_col, seg_count, seg_len, observed, obs_err):
    wide = block_weights(conv_w)
    lon_n = state.shape[0]
    lat_n = state.shape[1]
    flat = state.reshape(lon_n * lat_n, LEV, COLS, CH)

    def profile_of(column):
        feat = jax.nn.silu(conv_act(column, wide))
        return jnp.einsum('lcj,jn->cln', feat, readout, precision=lax.Precision.HIGHEST).reshape(COLS, LQ)

    profile = lax.map(profile_of, flat).reshape(lon_n, lat_n, COLS, LQ)
    rows_i = jnp.arange(lon_n, dtype=jnp.int32)[:, None, None]
    rows_j = jnp.arange(lat_n, dtype=jnp.int32)[None, :, None]
    weights = []
    total = jnp.zeros((lon_n, lat_n, RAYS_DEV, LQ), jnp.float32)
    for step in range(SPAN):
        counts = jnp.roll(seg_count, step, axis=0)
        weight = seg_len[:, :, step] * (counts > step).astype(jnp.float32)
        weights.append(weight)
        picked = profile[rows_i, rows_j, cross_col[:, :, step]] * weight[..., None]
        total = total + jnp.roll(picked, -step, axis=0)
    kflat = kernel.reshape(IMP, LQ)
    bending = jnp.einsum('ijrq,kq->ijrk', total, kflat, precision=lax.Precision.HIGHEST)
    adjoint = (bending - observed) / (obs_err * obs_err)
    projected = jnp.einsum('ijrk,kq->ijrq', adjoint, kflat, precision=lax.Precision.HIGHEST)
    dprofile = jnp.zeros((lon_n, lat_n, COLS, LQ), jnp.float32)
    for step in range(SPAN):
        values = jnp.roll(projected, step, axis=0) * weights[step][..., None]
        dprofile = dprofile.at[rows_i, rows_j, cross_col[:, :, step]].add(values)
    dflat = dprofile.reshape(lon_n * lat_n, COLS, LEV, NQ)

    def tile_back(pair):
        column, dprof = pair
        act = conv_act(column, wide)
        sig = jax.nn.sigmoid(act)
        dfeat = jnp.einsum('cln,jn->lcj', dprof, readout, precision=lax.Precision.HIGHEST)
        dact = (dfeat * sig * (1.0 + act * (1.0 - sig))).astype(jnp.bfloat16).astype(jnp.float32)
        dpad = jnp.pad(dact, ((1, 1), (0, 0), (0, 0)))
        xpad = jnp.pad(column.astype(jnp.float32), ((1, 1), (0, 0), (0, 0)))
        grad_x = jnp.zeros(act.shape, jnp.float32)
        grads = []
        for tap in range(KS):
            grad_x = grad_x + jnp.einsum('lcj,ij->lci', dpad[2 - tap:2 - tap + LEV], wide[tap], precision=lax.Precision.HIGHEST)
            grads.append(jnp.einsum('lci,lcj->ij', xpad[tap:tap + LEV], dact, precision=lax.Precision.HIGHEST))
        return grad_x.astype(jnp.bfloat16), jnp.stack(grads)

    grad_x, grad_w = lax.map(tile_back, (flat, dflat))
    grad_w = jnp.sum(grad_w, axis=0).reshape(KS, GROUPS, CG, GROUPS, CG)
    eye = jnp.eye(GROUPS, dtype=jnp.float32)
    grad_conv = jnp.einsum('tgahb,gh->tgab', grad_w, eye)
    return grad_x.reshape(state.shape), bending, grad_conv
```

```python
import functools

import jax
import jax.numpy as jnp
from jax import lax
from jax.experimental import pallas as pl
from jax.experimental.pallas import tpu as pltpu
from jax.sharding import PartitionSpec as P

F32 = jnp.float32
BF16 = jnp.bfloat16
LEV, COLS, CH, NQ, IMP, LQ = 64, 512, 128, 8, 256, 512
SPAN, HALF = 8, 128
CHUNK = 8
NCHUNK = LEV // CHUNK
MESH = pl.DeviceIdType.MESH

S_CNT, S_CC, S_SL, S_Z, S_FWD, S_BWD, S_DZ, S_R1, S_R2, S_R3, S_R4, S_N = (
    0, 10, 11, 12, 13, 23, 32, 33, 34, 42, 50, 51)


def split_hi_lo(value):
    hi = value.astype(BF16)
    return hi, (value - hi.astype(F32)).astype(BF16)


def iota(shape, dim):
    return lax.broadcasted_iota(jnp.int32, shape, dim)


def wide_tap(cw_ref, tap):
    flat = cw_ref[tap].astype(F32).reshape(CH, 16).astype(BF16)
    pick = jnp.where(iota((16, CH), 0) == lax.rem(iota((16, CH), 1), 16), 1.0, 0.0).astype(BF16)
    full = jnp.dot(flat, pick, preferred_element_type=F32)
    return jnp.where(iota((CH, CH), 0) // 16 == iota((CH, CH), 1) // 16, full, 0.0)


def level_matrix(cw_ref, out_ref, forward):
    taps = [wide_tap(cw_ref, t) for t in range(3)]
    for d in range(4):
        for p in range(2):
            t = d - p if forward else p + 2 - d
            if 0 <= t <= 2:
                block = taps[t] if forward else taps[t].T
            else:
                block = jnp.zeros((CH, CH), F32)
            out_ref[d * CH : (d + 1) * CH, p * CH : (p + 1) * CH] = block.astype(BF16)


def forward_kernel(
    state_ref, cw_ref, rt_ref, kt_ref, cc_ref, sc_ref, sl_ref, obs_ref, err_ref,
    bend_ref, da_out, gc_ref,
    xs, dsv, da, wf, wm, wr, kb, pacc, prof, cnt, cca, sla, zabs, own, ohf, ohb,
    msg, recv, adj, adjr, rhs, dzs, dzr, dpb, acc, g0, g1, g2, g3, fin,
    isem, osem, ssem, rsem,
):
    i = lax.axis_index("lon")
    j = lax.axis_index("lat")
    h = lax.rem(i, 2)
    p = i // 2
    sib = i + 1 - 2 * h

    def lon(u):
        return {"lon": lax.rem(u + 32, 16)}

    def copy(src, dst, s, r, dev):
        return pltpu.make_async_remote_copy(
            src_ref=src, dst_ref=dst, send_sem=ssem.at[s], recv_sem=rsem.at[r],
            device_id=dev, device_id_type=MESH)

    def arrived(dst, r):
        copy(dst, dst, r, r, lon(sib)).wait_recv()

    def load(c):
        return pltpu.make_async_copy(
            state_ref.at[pl.ds(c * CHUNK, CHUNK)], xs.at[pl.ds(1 + c * CHUNK, CHUNK)], isem.at[c])

    for c in range(NCHUNK):
        load(c).start()
    barrier = pltpu.get_barrier_semaphore()
    for d in range(1, 16):
        pl.semaphore_signal(barrier, inc=1, device_id=lon(i + d), device_id_type=MESH)
    for d in range(1, 8):
        pl.semaphore_signal(
            barrier, inc=1, device_id={"lat": lax.rem(j + d, 8)}, device_id_type=MESH)

    zero = jnp.zeros((COLS, CH), BF16)
    xs[0] = zero
    xs[LEV + 1] = zero
    da[0] = zero
    da[LEV + 1] = zero
    level_matrix(cw_ref, wf, True)
    tiled = jnp.concatenate([rt_ref[...]] * 16, axis=0)
    t_hi, t_lo = split_hi_lo(tiled)
    t_hi, t_lo = t_hi.astype(F32), t_lo.astype(F32)
    for m in range(8):
        for q in range(2):
            keep = iota((CH, CH), 1) // NQ == 2 * m + q
            rows = slice(m * 256 + q * 128, m * 256 + q * 128 + 128)
            wm[rows, 0:128] = jnp.where(keep, t_hi.T, 0.0).astype(BF16)
            wm[rows, 128:256] = jnp.where(keep, t_lo.T, 0.0).astype(BF16)
    t_mix = jnp.concatenate([t_hi[:64], t_lo[:64], t_hi[:64], t_lo[:64]], axis=0)
    for m in range(4):
        for q in range(2):
            keep = lax.rem(iota((256, CH), 0) // NQ, 8) == 2 * m + q
            wr[m * 256 : (m + 1) * 256, q * 128 : (q + 1) * 128] = jnp.where(
                keep, t_mix, 0.0).astype(BF16)
    kb_hi, kb_lo = split_hi_lo(kt_ref[...])
    kb[:, 0:256] = kb_hi
    kb[:, 256:512] = kb_lo

    pl.semaphore_wait(barrier, 22)
    cnt[1 - h] = sc_ref[...]
    cca[h] = cc_ref[...]
    sla[h] = sl_ref[...]
    early = [copy(sc_ref, cnt.at[1 - h], S_CNT, S_CNT + 1 - h, lon(sib)),
             copy(cc_ref, cca.at[h], S_CC, S_CC, lon(sib)),
             copy(sl_ref, sla.at[h], S_SL, S_SL, lon(sib))]
    for d in range(1, 5):
        for k in range(2):
            early.append(copy(sc_ref, cnt.at[2 * d + 1 - h], S_CNT + 2 * d - 1 + k,
                              S_CNT + 2 * d + 1 - h, lon(2 * (p + d) + k)))
    for c in early:
        c.start()

    for b in range(4):
        pacc[...] = jnp.zeros_like(pacc)
        if b == 0:
            load(0).wait()
        for half in range(2):
            chunk = 2 * b + half + 1
            if chunk < NCHUNK:
                load(chunk).wait()

            def pair(n, carry, b=b, half=half):
                k = half * 4 + n
                m = b * 8 + k
                x4 = jnp.concatenate([xs[2 * m + d] for d in range(4)], axis=1)
                act = jnp.dot(x4, wf[...], preferred_element_type=F32)
                sig = 0.5 * jnp.tanh(0.5 * act) + 0.5
                feat = act * sig
                slope = sig + feat * (1.0 - sig)
                dsv[2 * m] = slope[:, :128]
                dsv[2 * m + 1] = slope[:, 128:]
                pacc[...] += jnp.dot(feat.astype(BF16), wm[pl.ds(k * 256, 256), :],
                                     preferred_element_type=F32)
                return carry

            lax.fori_loop(0, 4, pair, 0)
        prof[:, b * 128 : (b + 1) * 128] = pacc[:, :128] + pacc[:, 128:]

    p_hi, p_lo = split_hi_lo(prof[...])
    zz = jnp.dot(p_hi, kb[...], preferred_element_type=F32)
    z = zz[:, :256] + zz[:, 256:] + jnp.dot(p_lo, kb[:, 0:256], preferred_element_type=F32)
    zabs[h] = z
    z_copy = copy(zabs.at[h], zabs.at[h], S_Z, S_Z, lon(sib))
    z_copy.start()

    arrived(cca.at[1 - h], S_CC)
    arrived(sla.at[1 - h], S_SL)
    arrived(cnt.at[h], S_CNT + h)
    for e in range(2, 10):
        arrived(cnt.at[e], S_CNT + e)

    def mine(row):
        return jnp.where(h == 0, row[:, :HALF], row[:, HALF:])

    cols_row = jnp.concatenate(
        [mine(cca[0]), mine(cca[1]), jnp.zeros((112, HALF), jnp.int32)], axis=0)
    weights = []
    for t in range(2):
        lens = mine(sla[t])
        for o in range(SPAN):
            count = mine(cnt[o + 1 - t])
            weights.append(lens[o : o + 1] * jnp.where(count > o, 1.0, 0.0))
    w_row = jnp.concatenate(weights + [jnp.zeros((112, HALF), F32)], axis=0)
    cols_t = cols_row.astype(F32).T.astype(jnp.int32)
    w_t = w_row.T
    lane_ids = iota((HALF, COLS), 1)
    row_ids = iota((COLS, HALF), 0)
    for t in range(2):
        for o in range(SPAN):
            k = t * SPAN + o
            ohf[t, o * HALF : (o + 1) * HALF, :] = jnp.where(
                lane_ids == cols_t[:, k : k + 1], 1.0, 0.0).astype(BF16)

    def gathered(t, o, zcat):
        got = jnp.dot(ohf[t, o * HALF : (o + 1) * HALF, :], zcat, preferred_element_type=F32)
        k = t * SPAN + o
        return (got[:, :256] + got[:, 256:]) * w_t[:, k : k + 1]

    arrived(zabs.at[1 - h], S_Z)
    zcats = [jnp.concatenate(split_hi_lo(zabs[t]), axis=1) for t in range(2)]
    fwd = {}
    for e in range(8, -1, -1):
        part = None
        if e >= 1:
            part = gathered(0, e - 1, zcats[0])
        if e <= 7:
            more = gathered(1, e, zcats[1])
            part = more if part is None else part + more
        msg[e] = part
        if e >= 2:
            d = e // 2
            fwd[e] = copy(msg.at[e], recv.at[2 * d + h], S_FWD + e, S_FWD + 2 * d + h,
                          lon(2 * p + 1 - e))
            fwd[e].start()
    near = copy(msg.at[h], recv.at[h], S_FWD, S_FWD + h, lon(sib))
    near.start()
    recv[h] = msg[1 - h]

    for t in range(2):
        for o in range(SPAN):
            k = t * SPAN + o
            ohb[t, :, o * HALF : (o + 1) * HALF] = jnp.where(
                row_ids == cols_row[k : k + 1, :], 1.0, 0.0).astype(BF16)

    arrived(recv.at[1 - h], S_FWD + 1 - h)
    for k in range(2, 8):
        arrived(recv.at[k], S_FWD + k)
    for s in range(2):
        adj[s] = recv[s] + recv[2 + s] + recv[4 + s] + recv[6 + s]

    @pl.when(h == 1)
    def _():
        for s in range(2):
            arrived(recv.at[8 + s], S_FWD + 8 + s)
            adj[s] += recv[8 + s]

    for s in range(2):
        rows = slice(s * HALF, (s + 1) * HALF)
        bent = adj[s]
        bend_ref[rows, :] = bent
        adj[s] = (bent - obs_ref[rows, :]) / (err_ref[rows, :] * err_ref[rows, :])

    bwd = []
    for d in range(3, 0, -1):
        for k in range(2):
            bwd.append(copy(adj.at[k], adjr.at[2 * d + 1 - h], S_BWD + 2 * d - 1 + k,
                            S_BWD + 2 * d + 1 - h, lon(2 * (p + d) + k)))
    last = [copy(adj.at[k], adjr.at[8], S_BWD + 7 + k, S_BWD + 8, lon(2 * (p + 4) + k))
            for k in range(2)]

    @pl.when(h == 1)
    def _():
        for c in last:
            c.start()

    for c in bwd:
        c.start()
    bnear = copy(adj.at[1 - h], adjr.at[1 - h], S_BWD, S_BWD + 1 - h, lon(sib))
    bnear.start()
    adjr[1 - h] = adj[h]

    arrived(adjr.at[h], S_BWD + h)
    for e in range(2, 9):
        arrived(adjr.at[e], S_BWD + e)

    for t in range(2):
        for o in range(SPAN):
            k = t * SPAN + o
            hi, lo = split_hi_lo(adjr[o + 1 - t] * w_t[:, k : k + 1])
            rhs[t, o * HALF : (o + 1) * HALF, 0:256] = hi
            rhs[t, o * HALF : (o + 1) * HALF, 256:512] = lo

    def scattered(t):
        got = jnp.dot(ohb[t], rhs[t], preferred_element_type=F32)
        return got[:, :256] + got[:, 256:]

    dzs[...] = scattered(1 - h)
    dz_copy = copy(dzs, dzr, S_DZ, S_DZ, lon(sib))
    dz_copy.start()
    mine_dz = scattered(h)
    arrived(dzr, S_DZ)
    d_hi, d_lo = split_hi_lo(mine_dz + dzr[...])
    contract = (((1,), (1,)), ((), ()))
    dprof = (lax.dot_general(d_hi, kb[:, 0:256], contract, preferred_element_type=F32)
             + lax.dot_general(d_lo, kb[:, 0:256], contract, preferred_element_type=F32)
             + lax.dot_general(d_hi, kb[:, 256:512], contract, preferred_element_type=F32))
    low = iota((COLS, 128), 1) < 64
    for b in range(4):
        part = dprof[:, b * 128 : (b + 1) * 128]
        other = pltpu.roll(part, 64, 1)
        for q in range(2):
            dup = jnp.where(low, part, other) if q == 0 else jnp.where(low, other, part)
            hi, lo = split_hi_lo(dup)
            dpb[2 * b + q, :, 0:128] = hi
            dpb[2 * b + q, :, 128:256] = lo

    def store(b):
        return pltpu.make_async_copy(
            da.at[pl.ds(8 * b + 1, 8)], da_out.at[pl.ds(8 * b, 8)], osem.at[b])

    for b in range(8):
        def slopes(m, carry, b=b):
            df = jnp.dot(dpb[b], wr[pl.ds(m * 256, 256), :], preferred_element_type=F32)
            l = 8 * b + 2 * m
            da[l + 1] = (df[:, :128] * dsv[l]).astype(BF16)
            da[l + 2] = (df[:, 128:] * dsv[l + 1]).astype(BF16)
            return carry

        lax.fori_loop(0, 4, slopes, 0, unroll=2)
        store(b).start()

    acc[...] = jnp.zeros_like(acc)

    def outer(m, carry):
        d4 = jnp.concatenate([da[2 * m + d] for d in range(4)], axis=1)
        x2 = jnp.concatenate([xs[2 * m + 1], xs[2 * m + 2]], axis=1)
        acc[...] += lax.dot_general(x2, d4, (((0,), (0,)), ((), ())), preferred_element_type=F32)
        return carry

    lax.fori_loop(0, 32, outer, 0, unroll=2)

    same = iota((CH, CH), 0) // 16 == iota((CH, CH), 1) // 16
    taps = []
    for t in range(3):
        full = (acc[0:128, (2 - t) * 128 : (3 - t) * 128]
                + acc[128:256, (3 - t) * 128 : (4 - t) * 128])
        taps.append(jnp.sum(jnp.where(same, full, 0.0).reshape(8, 16, CH), axis=0))
    flat = jnp.concatenate(taps, axis=0)
    g0[0] = flat[0:24]
    g0[1] = flat[24:48]
    r1 = copy(g0.at[1 - h], g1, S_R1, S_R1, lon(sib))
    r1.start()
    arrived(g1, S_R1)
    g2[p] = g0[h] + g1[...]
    r2 = [copy(g2.at[p], g2.at[p], S_R2 + d, S_R2 + p, lon(i + 2 * d)) for d in range(1, 8)]
    for c in r2:
        c.start()
    for d in range(1, 8):
        k = lax.rem(p + d, 8)
        arrived(g2.at[k], S_R2 + k)
    total = g2[0]
    for k in range(1, 8):
        total = total + g2[k]
    g3[j] = total
    r3 = [copy(g3.at[j], g3.at[j], S_R3 + d, S_R3 + j, {"lat": lax.rem(j + d, 8)})
          for d in range(1, 8)]
    for c in r3:
        c.start()
    for d in range(1, 8):
        k = lax.rem(j + d, 8)
        arrived(g3.at[k], S_R3 + k)
    total = g3[0]
    for k in range(1, 8):
        total = total + g3[k]
    fin[h] = total
    r4 = copy(fin.at[h], fin.at[h], S_R4, S_R4, lon(sib))
    r4.start()
    arrived(fin.at[1 - h], S_R4)
    gc_ref[0:24, :] = fin[0]
    gc_ref[24:48, :] = fin[1]

    for c in early + [z_copy, near] + list(fwd.values()) + bwd + [bnear, dz_copy, r1] + r2 + r3 + [r4]:
        c.wait_send()

    @pl.when(h == 1)
    def _():
        for c in last:
            c.wait_send()

    for b in range(8):
        store(b).wait()


def state_kernel(da_ref, cw_ref, out_ref, ds, gx, wb, isem, osem):
    def load(c):
        return pltpu.make_async_copy(
            da_ref.at[pl.ds(c * CHUNK, CHUNK)], ds.at[pl.ds(1 + c * CHUNK, CHUNK)], isem.at[c])

    def store(c):
        return pltpu.make_async_copy(
            gx.at[pl.ds(c * CHUNK, CHUNK)], out_ref.at[pl.ds(c * CHUNK, CHUNK)], osem.at[c])

    for c in range(NCHUNK):
        load(c).start()
    zero = jnp.zeros((COLS, CH), BF16)
    ds[0] = zero
    ds[LEV + 1] = zero
    level_matrix(cw_ref, wb, False)
    load(0).wait()
    for b in range(NCHUNK):
        if b + 1 < NCHUNK:
            load(b + 1).wait()

        def pair(n, carry, b=b):
            l = 8 * b + 2 * n
            d4 = jnp.concatenate([ds[l + d] for d in range(4)], axis=1)
            g = jnp.dot(d4, wb[...], preferred_element_type=F32)
            gx[l] = g[:, :128].astype(BF16)
            gx[l + 1] = g[:, 128:].astype(BF16)
            return carry

        lax.fori_loop(0, 4, pair, 0, unroll=2)
        store(b).start()
    for b in range(NCHUNK):
        store(b).wait()


def on_device(state, conv_w, readout, kernel, cross_col, seg_count, seg_len, observed, obs_err):
    vm = pl.BlockSpec(memory_space=pltpu.VMEM)
    hbm = pl.BlockSpec(memory_space=pl.ANY)
    sds = jax.ShapeDtypeStruct
    v = pltpu.VMEM
    dma = pltpu.SemaphoreType.DMA
    bending, dact, grad = pl.pallas_call(
        forward_kernel,
        out_shape=(sds((256, IMP), F32), sds((LEV, COLS, CH), BF16), sds((48, CH), F32)),
        in_specs=[hbm] + [vm] * 8,
        out_specs=(vm, hbm, vm),
        scratch_shapes=[
            v((LEV + 2, COLS, CH), BF16), v((LEV, COLS, CH), F32), v((LEV + 2, COLS, CH), BF16),
            v((512, 256), BF16), v((2048, 256), BF16), v((1024, 256), BF16), v((512, 512), BF16),
            v((512, 256), F32), v((512, 512), F32), v((10, 1, 256), jnp.int32),
            v((2, 8, 256), jnp.int32), v((2, 8, 256), F32), v((2, COLS, IMP), F32),
            v((8, 128), F32), v((2, 1024, 512), BF16), v((2, 512, 1024), BF16),
            v((9, HALF, IMP), F32), v((10, HALF, IMP), F32), v((2, HALF, IMP), F32),
            v((9, HALF, IMP), F32), v((2, 1024, 512), BF16), v((COLS, IMP), F32),
            v((COLS, IMP), F32), v((8, 512, 256), BF16), v((256, 512), F32),
            v((2, 24, CH), F32), v((24, CH), F32), v((8, 24, CH), F32), v((8, 24, CH), F32),
            v((2, 24, CH), F32),
            dma((NCHUNK,)), dma((NCHUNK,)), dma((S_N,)), dma((S_N,)),
        ],
        compiler_params=pltpu.CompilerParams(
            vmem_limit_bytes=60 << 20, collective_id=0, has_side_effects=True),
        name="bend",
    )(state[0, 0], conv_w, readout.T, kernel.transpose(1, 2, 0).reshape(LQ, IMP), cross_col[0, 0],
      seg_count[0], seg_len[0, 0], observed[0, 0], obs_err[0, 0])
    grad_x = pl.pallas_call(
        state_kernel,
        out_shape=sds((LEV, COLS, CH), BF16),
        in_specs=[hbm, vm],
        out_specs=hbm,
        scratch_shapes=[
            v((LEV + 2, COLS, CH), BF16), v((LEV, COLS, CH), BF16), v((512, 256), BF16),
            dma((NCHUNK,)), dma((NCHUNK,)),
        ],
        compiler_params=pltpu.CompilerParams(vmem_limit_bytes=40 << 20),
        name="gradx",
    )(dact, conv_w)
    grad_conv = grad.reshape(3, 16, 8, 16).transpose(0, 2, 1, 3)
    return grad_x[None, None], bending[None, None], grad_conv


def solution(mesh):
    in_specs = (
        P("lon", "lat", None, None, None),
        P(),
        P(),
        P(),
        P("lon", "lat", None, None),
        P("lon", "lat", None),
        P("lon", "lat", None, None),
        P("lon", "lat", None, None),
        P("lon", "lat", None, None),
    )
    out_specs = (P("lon", "lat", None, None, None), P("lon", "lat", None, None), P())
    return jax.shard_map(
        on_device, mesh=mesh, in_specs=in_specs, out_specs=out_specs, check_vma=False
    )
```

```python
import functools

import jax
import jax.numpy as jnp
from jax import lax
from jax.experimental import pallas as pl
from jax.experimental.pallas import tpu as pltpu
from jax.sharding import PartitionSpec as P

F32 = jnp.float32
BF16 = jnp.bfloat16
LEV, COLS, CH, NQ, IMP, LQ = 64, 512, 128, 8, 256, 512
SPAN, HALF = 8, 128
CHUNK = 8
NCHUNK = LEV // CHUNK
MESH = pl.DeviceIdType.MESH

PARTS = 2
RAYS = HALF // PARTS
S_CNT, S_CC, S_SL, S_DZ, S_NEAR, S_BNEAR, S_R1, S_R2, S_R3, S_R4 = (
    0, 10, 11, 12, 13, 15, 17, 18, 26, 34)
S_PART = 35
P_Z, P_FWD, P_FX, P_BX, P_BWD, P_N = 0, 1, 9, 11, 13, 22
S_N = S_PART + PARTS * P_N


def split_hi_lo(value):
    hi = value.astype(BF16)
    return hi, (value - hi.astype(F32)).astype(BF16)


def iota(shape, dim):
    return lax.broadcasted_iota(jnp.int32, shape, dim)


def wide_tap(cw_ref, tap):
    flat = cw_ref[tap].astype(F32).reshape(CH, 16).astype(BF16)
    pick = jnp.where(iota((16, CH), 0) == lax.rem(iota((16, CH), 1), 16), 1.0, 0.0).astype(BF16)
    full = jnp.dot(flat, pick, preferred_element_type=F32)
    return jnp.where(iota((CH, CH), 0) // 16 == iota((CH, CH), 1) // 16, full, 0.0)


def level_matrix(cw_ref, out_ref, forward):
    taps = [wide_tap(cw_ref, t) for t in range(3)]
    for d in range(4):
        for p in range(2):
            t = d - p if forward else p + 2 - d
            if 0 <= t <= 2:
                block = taps[t] if forward else taps[t].T
            else:
                block = jnp.zeros((CH, CH), F32)
            out_ref[d * CH : (d + 1) * CH, p * CH : (p + 1) * CH] = block.astype(BF16)


def forward_kernel(
    state_ref, cw_ref, rt_ref, kt_ref, cc_ref, sc_ref, sl_ref, obs_ref, err_ref,
    bend_ref, gx_out, gc_ref,
    xs, dsv, da, wf, wb, wm, wr, kb, pacc, prof, acts, feats, cnt, cca, sla, zabs, ohf, ohb,
    msg, recv, rel, xr, adx, adjr, rhs, dzs, dzr, dpb, acc, g0, g1, g2, g3, fin,
    isem, osem, ssem, rsem,
):
    i = lax.axis_index("lon")
    j = lax.axis_index("lat")
    h = lax.rem(i, 2)
    p = i // 2
    row = lax.rem(p, 4)
    column = p // 4
    sib = i + 1 - 2 * h

    def lon(u):
        return {"lon": lax.rem(u + 32, 16)}

    def copy(src, dst, s, r, dev):
        return pltpu.make_async_remote_copy(
            src_ref=src, dst_ref=dst, send_sem=ssem.at[s], recv_sem=rsem.at[r],
            device_id=dev, device_id_type=MESH)

    def arrived(dst, r):
        copy(dst, dst, r, r, lon(sib)).wait_recv()

    def load(c):
        return pltpu.make_async_copy(
            state_ref.at[pl.ds(c * CHUNK, CHUNK)], xs.at[pl.ds(1 + c * CHUNK, CHUNK)], isem.at[c])

    for c in range(NCHUNK):
        load(c).start()
    barrier = pltpu.get_barrier_semaphore()
    for d in range(1, 16):
        pl.semaphore_signal(barrier, inc=1, device_id=lon(i + d), device_id_type=MESH)
    for d in range(1, 8):
        pl.semaphore_signal(
            barrier, inc=1, device_id={"lat": lax.rem(j + d, 8)}, device_id_type=MESH)

    zero = jnp.zeros((COLS, CH), BF16)
    xs[0] = zero
    xs[LEV + 1] = zero
    da[0] = zero
    da[LEV + 1] = zero
    level_matrix(cw_ref, wf, True)
    tiled = jnp.concatenate([rt_ref[...]] * 16, axis=0)
    t_hi, t_lo = split_hi_lo(tiled)
    t_hi, t_lo = t_hi.astype(F32), t_lo.astype(F32)
    for m in range(8):
        for q in range(2):
            keep = iota((CH, CH), 1) // NQ == 2 * m + q
            rows = slice(m * 256 + q * 128, m * 256 + q * 128 + 128)
            wm[rows, 0:128] = jnp.where(keep, t_hi.T, 0.0).astype(BF16)
            wm[rows, 128:256] = jnp.where(keep, t_lo.T, 0.0).astype(BF16)
    def convolve(m):
        x4 = jnp.concatenate([xs[2 * m + d] for d in range(4)], axis=1)
        return jnp.dot(x4, wf[...], preferred_element_type=F32)

    def activate(k, m):
        act = acts[k][...]
        sig = 0.5 * jnp.tanh(0.5 * act) + 0.5
        feat = act * sig
        slope = sig + feat * (1.0 - sig)
        dsv[2 * m] = slope[:, :128]
        dsv[2 * m + 1] = slope[:, 128:]
        feats[k][...] = feat.astype(BF16)

    def read_out(a, k):
        both = jnp.concatenate([feats[a][...], feats[a + 1][...]], axis=1)
        pacc[...] += jnp.dot(both, wm[pl.ds(k * 256, 512), :], preferred_element_type=F32)

    early = [copy(sc_ref, cnt.at[1 - h], S_CNT, S_CNT + 1 - h, lon(sib)),
             copy(cc_ref, cca.at[h], S_CC, S_CC, lon(sib)),
             copy(sl_ref, sla.at[h], S_SL, S_SL, lon(sib))]
    for d in range(1, 5):
        for k in range(2):
            early.append(copy(sc_ref, cnt.at[2 * d + 1 - h], S_CNT + 2 * d - 1 + k,
                              S_CNT + 2 * d + 1 - h, lon(2 * (p + d) + k)))
    pending = list(early)
    cnt[1 - h] = sc_ref[...]
    cca[h] = cc_ref[...]
    sla[h] = sl_ref[...]

    load(0).wait()
    acts[0][...] = convolve(0)
    acts[1][...] = convolve(1)
    for b in range(4):
        pacc[...] = jnp.zeros_like(pacc)
        for half in range(2):
            if (b, half) == (2, 0):
                pl.semaphore_wait(barrier, 22)
                for c in early:
                    c.start()
            ahead = 2 * b + half + 1
            if ahead < NCHUNK:
                load(ahead).wait()
            m = b * 8 + half * 4
            acts[2][...] = convolve(m + 2)
            activate(0, m)
            acts[3][...] = convolve(m + 3)
            activate(1, m + 1)
            read_out(0, 4 * half)
            if m + 4 < 32:
                acts[0][...] = convolve(m + 4)
            activate(2, m + 2)
            if m + 5 < 32:
                acts[1][...] = convolve(m + 5)
            activate(3, m + 3)
            read_out(2, 4 * half + 2)
        prof[:, b * 128 : (b + 1) * 128] = pacc[:, :128] + pacc[:, 128:]

    kb_hi, kb_lo = split_hi_lo(kt_ref[...])
    kb[:, 0:256] = kb_hi
    kb[:, 256:512] = kb_lo
    p_hi, p_lo = split_hi_lo(prof[...])
    zz = jnp.dot(p_hi, kb[...], preferred_element_type=F32)
    zabs[h] = zz[:, :256] + zz[:, 256:] + jnp.dot(p_lo, kb[:, 0:256], preferred_element_type=F32)
    z_copy = copy(zabs.at[h], zabs.at[h], S_PART + P_Z, S_PART + P_Z, lon(sib))
    z_copy.start()
    pending.append(z_copy)

    arrived(cca.at[1 - h], S_CC)
    arrived(sla.at[1 - h], S_SL)
    arrived(cnt.at[h], S_CNT + h)
    for e in range(2, 10):
        arrived(cnt.at[e], S_CNT + e)

    def mine(row):
        return jnp.where(h == 0, row[:, :HALF], row[:, HALF:])

    cols_row = jnp.concatenate(
        [mine(cca[0]), mine(cca[1]), jnp.zeros((112, HALF), jnp.int32)], axis=0)
    weights = []
    for t in range(2):
        lens = mine(sla[t])
        for o in range(SPAN):
            count = mine(cnt[o + 1 - t])
            weights.append(lens[o : o + 1] * jnp.where(count > o, 1.0, 0.0))
    w_row = jnp.concatenate(weights + [jnp.zeros((112, HALF), F32)], axis=0)
    cols_t = cols_row.astype(F32).T.astype(jnp.int32)
    w_t = w_row.T
    lane_ids = iota((HALF, COLS), 1)
    row_ids = iota((COLS, HALF), 0)
    for t in range(2):
        for o in range(SPAN):
            k = t * SPAN + o
            for c in range(PARTS):
                ohf[t, (c * SPAN + o) * RAYS : (c * SPAN + o + 1) * RAYS, :] = jnp.where(
                    lane_ids[:RAYS] == cols_t[c * RAYS : (c + 1) * RAYS, k : k + 1], 1.0, 0.0
                ).astype(BF16)

    def gathered(t, c, zcat):
        got = jnp.dot(ohf[t, c * SPAN * RAYS : (c + 1) * SPAN * RAYS, :], zcat,
                      preferred_element_type=F32)
        got = got[:, :256] + got[:, 256:]
        return [got[o * RAYS : (o + 1) * RAYS]
                * w_t[c * RAYS : (c + 1) * RAYS, t * SPAN + o : t * SPAN + o + 1]
                for o in range(SPAN)]

    arrived(zabs.at[1 - h], S_PART + P_Z)
    zcats = [jnp.concatenate(split_hi_lo(zabs[t]), axis=1) for t in range(2)]
    other = 8 * (1 - column) + 2 * row

    def push(c):
        cut = pl.ds(c * RAYS, RAYS)
        base = S_PART + c * P_N
        first, second = gathered(0, c, zcats[0]), gathered(1, c, zcats[1])
        for d in range(3, 0, -1):
            direct = row >= d
            across = 8 * column + 2 * lax.rem(row - d + 4, 4) + h
            for k in range(2):
                e = 2 * d + 1 - k
                msg[e, cut, :] = first[e - 1] + second[e]
                target = jnp.where(direct, 2 * (p - d) + k, across)
                slot = 2 * d + jnp.where(direct, h, k)
                send = copy(msg.at[e, cut], recv.at[slot, cut], base + P_FWD + e,
                            base + P_FWD + slot, lon(target))
                send.start()
                pending.append(send)
        msg[1, cut, :] = first[0] + second[1]
        msg[0, cut, :] = second[0]
        rel[0, cut, :] = jnp.zeros((RAYS, IMP), F32)
        rel[1, cut, :] = first[7]
        near = copy(msg.at[h, cut], recv.at[h, cut], S_NEAR + c, base + P_FWD + h, lon(sib))
        near.start()
        pending.append(near)
        recv[h, cut, :] = msg[1 - h, cut, :]

    cross, bcross, spread = {}, {}, {}

    def relay(c):
        cut = pl.ds(c * RAYS, RAYS)
        base = S_PART + c * P_N
        for d in range(3, 0, -1):
            @pl.when(row + d > 3)
            def _(d=d):
                for k in range(2):
                    arrived(recv.at[2 * d + k, cut], base + P_FWD + 2 * d + k)
                    rel[k, cut, :] += recv[2 * d + k, cut, :]

        for k in range(2):
            cross[c, k] = copy(rel.at[k, cut], xr.at[h, cut], base + P_FX + k, base + P_FX + h,
                               lon(other + k))
        cross[c, 1].start()
        pending.append(cross[c, 1])

        @pl.when(row > 0)
        def _():
            cross[c, 0].start()

    def own(c):
        cut = pl.ds(c * RAYS, RAYS)
        base = S_PART + c * P_N
        arrived(recv.at[1 - h, cut], base + P_FWD + 1 - h)
        for s in range(2):
            adx[s, cut, :] = recv[s, cut, :]
        for d in range(1, 4):
            @pl.when(row + d <= 3)
            def _(d=d):
                for s in range(2):
                    arrived(recv.at[2 * d + s, cut], base + P_FWD + 2 * d + s)
                    adx[s, cut, :] += recv[2 * d + s, cut, :]

        @pl.when(row + h > 0)
        def _():
            for s in range(2):
                arrived(xr.at[s, cut], base + P_FX + s)
                adx[s, cut, :] += xr[s, cut, :]

        for s in range(2):
            rows = slice(s * HALF + c * RAYS, s * HALF + (c + 1) * RAYS)
            bent = adx[s, cut, :]
            bend_ref[rows, :] = bent
            adx[s, cut, :] = (bent - obs_ref[rows, :]) / (err_ref[rows, :] * err_ref[rows, :])
        for s in range(2):
            bcross[c, s] = copy(adx.at[s, cut], adx.at[2 + h, cut], base + P_BX + s,
                                base + P_BX + h, lon(other + s))

        @pl.when(row + h > 0)
        def _():
            bcross[c, 0].start()
            bcross[c, 1].start()

        for d in range(1, 4):
            direct = row + d <= 3
            below = 8 * column + 2 * lax.rem(row + d, 4)
            for k in range(2):
                e = 2 * d + 1 - jnp.where(direct, h, k)
                spread[c, d, k] = copy(
                    adx.at[jnp.where(direct, k, 2 + k), cut], adjr.at[e, cut],
                    base + P_BWD + 2 * d - 1 + k, base + P_BWD + e,
                    lon(below + jnp.where(direct, k, h)))
                pending.append(spread[c, d, k])
        for d in range(3, 0, -1):
            @pl.when(row + d <= 3)
            def _(d=d):
                spread[c, d, 0].start()
                spread[c, d, 1].start()
        bnear = copy(adx.at[1 - h, cut], adjr.at[1 - h, cut], S_BNEAR + c, base + P_BWD + 1 - h,
                     lon(sib))
        bnear.start()
        pending.append(bnear)
        adjr[1 - h, cut, :] = adx[h, cut, :]

    def pass_on(c):
        cut = pl.ds(c * RAYS, RAYS)
        base = S_PART + c * P_N

        @pl.when(row > 0)
        def _():
            arrived(adx.at[2, cut], base + P_BX)

        arrived(adx.at[3, cut], base + P_BX + 1)
        for d in range(3, 0, -1):
            @pl.when(row + d > 3)
            def _(d=d):
                spread[c, d, 0].start()
                spread[c, d, 1].start()
        adjr[8, cut, :] = adx[3, cut, :]

    push(0)
    push(1)
    for t in range(2):
        for o in range(SPAN):
            k = t * SPAN + o
            ohb[t, :, o * HALF : (o + 1) * HALF] = jnp.where(
                row_ids == cols_row[k : k + 1, :], 1.0, 0.0).astype(BF16)
    level_matrix(cw_ref, wb, False)
    t_mix = jnp.concatenate([t_hi[:64], t_lo[:64], t_hi[:64], t_lo[:64]], axis=0)
    for m in range(4):
        for q in range(2):
            keep = lax.rem(iota((256, CH), 0) // NQ, 8) == 2 * m + q
            wr[m * 256 : (m + 1) * 256, q * 128 : (q + 1) * 128] = jnp.where(
                keep, t_mix, 0.0).astype(BF16)
    relay(0)
    own(0)
    relay(1)
    pass_on(0)
    own(1)
    pass_on(1)
    for c in range(PARTS):
        cut = pl.ds(c * RAYS, RAYS)
        base = S_PART + c * P_N + P_BWD
        arrived(adjr.at[h, cut], base + h)
        for e in range(2, 8):
            arrived(adjr.at[e, cut], base + e)

    for t in range(2):
        for o in range(SPAN):
            k = t * SPAN + o
            hi, lo = split_hi_lo(adjr[o + 1 - t] * w_t[:, k : k + 1])
            rhs[t, o * HALF : (o + 1) * HALF, 0:256] = hi
            rhs[t, o * HALF : (o + 1) * HALF, 256:512] = lo

    def scattered(t):
        got = jnp.dot(ohb[t], rhs[t], preferred_element_type=F32)
        return got[:, :256] + got[:, 256:]

    dzs[...] = scattered(1 - h)
    dz_copy = copy(dzs, dzr, S_DZ, S_DZ, lon(sib))
    dz_copy.start()
    pending.append(dz_copy)
    mine_dz = scattered(h)
    arrived(dzr, S_DZ)
    d_hi, d_lo = split_hi_lo(mine_dz + dzr[...])
    contract = (((1,), (1,)), ((), ()))
    dprof = (lax.dot_general(d_hi, kb[:, 0:256], contract, preferred_element_type=F32)
             + lax.dot_general(d_lo, kb[:, 0:256], contract, preferred_element_type=F32)
             + lax.dot_general(d_hi, kb[:, 256:512], contract, preferred_element_type=F32))
    low = iota((COLS, 128), 1) < 64
    for b in range(4):
        part = dprof[:, b * 128 : (b + 1) * 128]
        other = pltpu.roll(part, 64, 1)
        for q in range(2):
            dup = jnp.where(low, part, other) if q == 0 else jnp.where(low, other, part)
            hi, lo = split_hi_lo(dup)
            dpb[2 * b + q, :, 0:128] = hi
            dpb[2 * b + q, :, 128:256] = lo

    def store(b):
        return pltpu.make_async_copy(
            xs.at[pl.ds(8 * b + 1, 8)], gx_out.at[pl.ds(8 * b, 8)], osem.at[b])

    for b in range(8):
        def slopes(m, carry, b=b):
            df = jnp.dot(dpb[b], wr[pl.ds(m * 256, 256), :], preferred_element_type=F32)
            l = 8 * b + 2 * m
            da[l + 1] = (df[:, :128] * dsv[l]).astype(BF16)
            da[l + 2] = (df[:, 128:] * dsv[l + 1]).astype(BF16)
            return carry

        lax.fori_loop(0, 4, slopes, 0, unroll=2)

    acc[...] = jnp.zeros_like(acc)

    def outer(m, carry):
        d4 = jnp.concatenate([da[2 * m + d] for d in range(4)], axis=1)
        x2 = jnp.concatenate([xs[2 * m + 1], xs[2 * m + 2]], axis=1)
        acc[...] += lax.dot_general(x2, d4, (((0,), (0,)), ((), ())), preferred_element_type=F32)
        return carry

    lax.fori_loop(0, 32, outer, 0, unroll=2)

    def state_levels(b):
        def pair(n, carry):
            l = 8 * b + 2 * n
            d4 = jnp.concatenate([da[l + d] for d in range(4)], axis=1)
            g = jnp.dot(d4, wb[...], preferred_element_type=F32)
            xs[l + 1] = g[:, :128].astype(BF16)
            xs[l + 2] = g[:, 128:].astype(BF16)
            return carry

        lax.fori_loop(0, 4, pair, 0, unroll=2)
        store(b).start()

    same = iota((CH, CH), 0) // 16 == iota((CH, CH), 1) // 16
    taps = []
    for t in range(3):
        full = (acc[0:128, (2 - t) * 128 : (3 - t) * 128]
                + acc[128:256, (3 - t) * 128 : (4 - t) * 128])
        taps.append(jnp.sum(jnp.where(same, full, 0.0).reshape(8, 16, CH), axis=0))
    flat = jnp.concatenate(taps, axis=0)
    g0[0] = flat[0:24]
    g0[1] = flat[24:48]
    r1 = copy(g0.at[1 - h], g1, S_R1, S_R1, lon(sib))
    r1.start()
    pending.append(r1)
    state_levels(0)
    state_levels(1)
    arrived(g1, S_R1)
    g2[p] = g0[h] + g1[...]
    r2 = [copy(g2.at[p], g2.at[p], S_R2 + d, S_R2 + p, lon(i + 2 * d)) for d in range(1, 8)]
    for c in r2:
        c.start()
    pending.extend(r2)
    state_levels(2)
    state_levels(3)
    state_levels(4)
    for d in range(1, 8):
        k = lax.rem(p + d, 8)
        arrived(g2.at[k], S_R2 + k)
    total = g2[0]
    for k in range(1, 8):
        total = total + g2[k]
    g3[j] = total
    r3 = [copy(g3.at[j], g3.at[j], S_R3 + d, S_R3 + j, {"lat": lax.rem(j + d, 8)})
          for d in range(1, 8)]
    for c in r3:
        c.start()
    pending.extend(r3)
    state_levels(5)
    state_levels(6)
    for d in range(1, 8):
        k = lax.rem(j + d, 8)
        arrived(g3.at[k], S_R3 + k)
    total = g3[0]
    for k in range(1, 8):
        total = total + g3[k]
    fin[h] = total
    r4 = copy(fin.at[h], fin.at[h], S_R4, S_R4, lon(sib))
    r4.start()
    pending.append(r4)
    state_levels(7)
    arrived(fin.at[1 - h], S_R4)
    gc_ref[0:24, :] = fin[0]
    gc_ref[24:48, :] = fin[1]

    for c in pending:
        c.wait_send()

    @pl.when(row > 0)
    def _():
        for c in range(PARTS):
            cross[c, 0].wait_send()

    @pl.when(row + h > 0)
    def _():
        for c in range(PARTS):
            bcross[c, 0].wait_send()
            bcross[c, 1].wait_send()

    for b in range(8):
        store(b).wait()


def on_device(state, conv_w, readout, kernel, cross_col, seg_count, seg_len, observed, obs_err):
    vm = pl.BlockSpec(memory_space=pltpu.VMEM)
    hbm = pl.BlockSpec(memory_space=pl.ANY)
    sds = jax.ShapeDtypeStruct
    v = pltpu.VMEM
    dma = pltpu.SemaphoreType.DMA
    bending, grad_x, grad = pl.pallas_call(
        forward_kernel,
        out_shape=(sds((256, IMP), F32), sds((LEV, COLS, CH), BF16), sds((48, CH), F32)),
        in_specs=[hbm] + [vm] * 8,
        out_specs=(vm, hbm, vm),
        scratch_shapes=[
            v((LEV + 2, COLS, CH), BF16), v((LEV, COLS, CH), F32), v((LEV + 2, COLS, CH), BF16),
            v((512, 256), BF16), v((512, 256), BF16), v((2048, 256), BF16), v((1024, 256), BF16),
            v((512, 512), BF16), v((512, 256), F32), v((512, 512), F32),
            [v((512, 256), F32)] * 4, [v((512, 256), BF16)] * 4, v((10, 1, 256), jnp.int32),
            v((2, 8, 256), jnp.int32), v((2, 8, 256), F32), v((2, COLS, IMP), F32),
            v((2, 1024, 512), BF16), v((2, 512, 1024), BF16),
            v((9, HALF, IMP), F32), v((8, HALF, IMP), F32), v((2, HALF, IMP), F32),
            v((2, HALF, IMP), F32), v((4, HALF, IMP), F32), v((9, HALF, IMP), F32), v((2, 1024, 512), BF16), v((COLS, IMP), F32),
            v((COLS, IMP), F32), v((8, 512, 256), BF16), v((256, 512), F32),
            v((2, 24, CH), F32), v((24, CH), F32), v((8, 24, CH), F32), v((8, 24, CH), F32),
            v((2, 24, CH), F32),
            dma((NCHUNK,)), dma((NCHUNK,)), dma((S_N,)), dma((S_N,)),
        ],
        compiler_params=pltpu.CompilerParams(
            vmem_limit_bytes=60 << 20, collective_id=0, has_side_effects=True),
        name="bend",
    )(state[0, 0], conv_w, readout.T, kernel.transpose(1, 2, 0).reshape(LQ, IMP), cross_col[0, 0],
      seg_count[0], seg_len[0, 0], observed[0, 0], obs_err[0, 0])
    grad_conv = grad.reshape(3, 16, 8, 16).transpose(0, 2, 1, 3)
    return grad_x[None, None], bending[None, None], grad_conv


def solution(mesh):
    in_specs = (
        P("lon", "lat", None, None, None),
        P(),
        P(),
        P(),
        P("lon", "lat", None, None),
        P("lon", "lat", None),
        P("lon", "lat", None, None),
        P("lon", "lat", None, None),
        P("lon", "lat", None, None),
    )
    out_specs = (P("lon", "lat", None, None, None), P("lon", "lat", None, None), P())
    return jax.shard_map(
        on_device, mesh=mesh, in_specs=in_specs, out_specs=out_specs, check_vma=False
    )
```

```python
import functools

import jax
import jax.numpy as jnp
from jax import lax
from jax.experimental import pallas as pl
from jax.experimental.pallas import tpu as pltpu
from jax.sharding import PartitionSpec as P

F32 = jnp.float32
BF16 = jnp.bfloat16
LEV, COLS, CH, NQ, IMP, LQ = 64, 512, 128, 8, 256, 512
SPAN, HALF = 8, 128
CHUNK = 8
NCHUNK = LEV // CHUNK
MESH = pl.DeviceIdType.MESH

PARTS = 2
RAYS = HALF // PARTS
S_CNT, S_CC, S_SL, S_DZ, S_NEAR, S_BNEAR, S_R1, S_R2, S_PART = 0, 10, 11, 12, 13, 17, 21, 37, 53
P_Z, P_FWD, P_FX, P_BX, P_BWD, P_N = 0, 1, 9, 11, 13, 22
S_N = S_PART + PARTS * P_N


def split_hi_lo(value):
    hi = value.astype(BF16)
    return hi, (value - hi.astype(F32)).astype(BF16)


def iota(shape, dim):
    return lax.broadcasted_iota(jnp.int32, shape, dim)


def wide_tap(cw_ref, tap):
    flat = cw_ref[tap].astype(F32).reshape(CH, 16).astype(BF16)
    pick = jnp.where(iota((16, CH), 0) == lax.rem(iota((16, CH), 1), 16), 1.0, 0.0).astype(BF16)
    full = jnp.dot(flat, pick, preferred_element_type=F32)
    return jnp.where(iota((CH, CH), 0) // 16 == iota((CH, CH), 1) // 16, full, 0.0)


def level_matrix(cw_ref, out_ref, forward):
    taps = [wide_tap(cw_ref, t) for t in range(3)]
    for d in range(4):
        for p in range(2):
            t = d - p if forward else p + 2 - d
            if 0 <= t <= 2:
                block = taps[t] if forward else taps[t].T
            else:
                block = jnp.zeros((CH, CH), F32)
            out_ref[d * CH : (d + 1) * CH, p * CH : (p + 1) * CH] = block.astype(BF16)


def forward_kernel(
    state_ref, cw_ref, rt_ref, kt_ref, cc_ref, sc_ref, sl_ref, obs_ref, err_ref,
    bend_ref, gx_out, gc_ref,
    xs, dsv, da, wf, wb, wm, wr, kb, pacc, prof, acts, feats, cnt, cca, sla, zabs, ohf, ohb,
    msg, recv, rel, xr, adx, adjr, rhs, dzs, dzm, dzr, dpb, acc, g0, g1, g2,
    isem, osem, ssem, rsem,
):
    i = lax.axis_index("lon")
    j = lax.axis_index("lat")
    h = lax.rem(i, 2)
    p = i // 2
    row = lax.rem(p, 4)
    column = p // 4
    sib = i + 1 - 2 * h

    def lon(u):
        return {"lon": lax.rem(u + 32, 16)}

    def copy(src, dst, s, r, dev):
        return pltpu.make_async_remote_copy(
            src_ref=src, dst_ref=dst, send_sem=ssem.at[s], recv_sem=rsem.at[r],
            device_id=dev, device_id_type=MESH)

    def arrived(dst, r):
        copy(dst, dst, r, r, lon(sib)).wait_recv()

    def load(c):
        return pltpu.make_async_copy(
            state_ref.at[pl.ds(c * CHUNK, CHUNK)], xs.at[pl.ds(1 + c * CHUNK, CHUNK)], isem.at[c])

    for c in range(NCHUNK):
        load(c).start()
    barrier = pltpu.get_barrier_semaphore()
    for d in range(1, 16):
        pl.semaphore_signal(barrier, inc=1, device_id=lon(i + d), device_id_type=MESH)
    for d in range(1, 8):
        for u in (i, sib):
            pl.semaphore_signal(barrier, inc=1, device_id={"lon": u, "lat": lax.rem(j + d, 8)},
                                device_id_type=MESH)

    zero = jnp.zeros((COLS, CH), BF16)
    xs[0] = zero
    xs[LEV + 1] = zero
    da[0] = zero
    da[LEV + 1] = zero
    level_matrix(cw_ref, wf, True)
    tiled = jnp.concatenate([rt_ref[...]] * 16, axis=0)
    t_hi, t_lo = split_hi_lo(tiled)
    t_hi, t_lo = t_hi.astype(F32), t_lo.astype(F32)
    for m in range(8):
        for q in range(2):
            keep = iota((CH, CH), 1) // NQ == 2 * m + q
            rows = slice(m * 256 + q * 128, m * 256 + q * 128 + 128)
            wm[rows, 0:128] = jnp.where(keep, t_hi.T, 0.0).astype(BF16)
            wm[rows, 128:256] = jnp.where(keep, t_lo.T, 0.0).astype(BF16)
    def convolve(m):
        x4 = jnp.concatenate([xs[2 * m + d] for d in range(4)], axis=1)
        return jnp.dot(x4, wf[...], preferred_element_type=F32)

    def activate(k, m):
        act = acts[k][...]
        sig = 0.5 * jnp.tanh(0.5 * act) + 0.5
        feat = act * sig
        slope = sig + feat * (1.0 - sig)
        dsv[2 * m] = slope[:, :128]
        dsv[2 * m + 1] = slope[:, 128:]
        feats[k][...] = feat.astype(BF16)

    def read_out(a, k):
        both = jnp.concatenate([feats[a][...], feats[a + 1][...]], axis=1)
        pacc[...] += jnp.dot(both, wm[pl.ds(k * 256, 512), :], preferred_element_type=F32)

    early = [copy(sc_ref, cnt.at[1 - h], S_CNT, S_CNT + 1 - h, lon(sib)),
             copy(cc_ref, cca.at[h], S_CC, S_CC, lon(sib)),
             copy(sl_ref, sla.at[h], S_SL, S_SL, lon(sib))]
    for d in range(1, 5):
        for k in range(2):
            early.append(copy(sc_ref, cnt.at[2 * d + 1 - h], S_CNT + 2 * d - 1 + k,
                              S_CNT + 2 * d + 1 - h, lon(2 * (p + d) + k)))
    pending = list(early)
    cnt[1 - h] = sc_ref[...]
    cca[h] = cc_ref[...]
    sla[h] = sl_ref[...]

    load(0).wait()
    acts[0][...] = convolve(0)
    acts[1][...] = convolve(1)
    for b in range(4):
        pacc[...] = jnp.zeros_like(pacc)
        for half in range(2):
            if (b, half) == (2, 0):
                pl.semaphore_wait(barrier, 29)
                for c in early:
                    c.start()
            ahead = 2 * b + half + 1
            if ahead < NCHUNK:
                load(ahead).wait()
            m = b * 8 + half * 4
            acts[2][...] = convolve(m + 2)
            activate(0, m)
            acts[3][...] = convolve(m + 3)
            activate(1, m + 1)
            read_out(0, 4 * half)
            if m + 4 < 32:
                acts[0][...] = convolve(m + 4)
            activate(2, m + 2)
            if m + 5 < 32:
                acts[1][...] = convolve(m + 5)
            activate(3, m + 3)
            read_out(2, 4 * half + 2)
        prof[:, b * 128 : (b + 1) * 128] = pacc[:, :128] + pacc[:, 128:]

    kb_hi, kb_lo = split_hi_lo(kt_ref[...])
    kb[:, 0:256] = kb_hi
    kb[:, 256:512] = kb_lo
    p_hi, p_lo = split_hi_lo(prof[...])
    zz = jnp.dot(p_hi, kb[...], preferred_element_type=F32)
    zabs[h] = zz[:, :256] + zz[:, 256:] + jnp.dot(p_lo, kb[:, 0:256], preferred_element_type=F32)
    z_copy = copy(zabs.at[h], zabs.at[h], S_PART + P_Z, S_PART + P_Z, lon(sib))
    z_copy.start()
    pending.append(z_copy)

    arrived(cca.at[1 - h], S_CC)
    arrived(sla.at[1 - h], S_SL)
    arrived(cnt.at[h], S_CNT + h)
    for e in range(2, 10):
        arrived(cnt.at[e], S_CNT + e)

    def mine(row):
        return jnp.where(h == 0, row[:, :HALF], row[:, HALF:])

    cols_row = jnp.concatenate(
        [mine(cca[0]), mine(cca[1]), jnp.zeros((112, HALF), jnp.int32)], axis=0)
    weights = []
    for t in range(2):
        lens = mine(sla[t])
        for o in range(SPAN):
            count = mine(cnt[o + 1 - t])
            weights.append(lens[o : o + 1] * jnp.where(count > o, 1.0, 0.0))
    w_row = jnp.concatenate(weights + [jnp.zeros((112, HALF), F32)], axis=0)
    cols_t = cols_row.astype(F32).T.astype(jnp.int32)
    w_t = w_row.T
    lane_ids = iota((HALF, COLS), 1)
    row_ids = iota((COLS, HALF), 0)
    for t in range(2):
        for o in range(SPAN):
            k = t * SPAN + o
            for c in range(PARTS):
                ohf[t, (c * SPAN + o) * RAYS : (c * SPAN + o + 1) * RAYS, :] = jnp.where(
                    lane_ids[:RAYS] == cols_t[c * RAYS : (c + 1) * RAYS, k : k + 1], 1.0, 0.0
                ).astype(BF16)

    def gathered(t, c, zcat):
        got = jnp.dot(ohf[t, c * SPAN * RAYS : (c + 1) * SPAN * RAYS, :], zcat,
                      preferred_element_type=F32)
        got = got[:, :256] + got[:, 256:]
        return [got[o * RAYS : (o + 1) * RAYS]
                * w_t[c * RAYS : (c + 1) * RAYS, t * SPAN + o : t * SPAN + o + 1]
                for o in range(SPAN)]

    arrived(zabs.at[1 - h], S_PART + P_Z)
    zcats = [jnp.concatenate(split_hi_lo(zabs[t]), axis=1) for t in range(2)]
    other = 8 * (1 - column) + 2 * row

    def push(c):
        cut = pl.ds(c * RAYS, RAYS)
        base = S_PART + c * P_N
        first, second = gathered(0, c, zcats[0]), gathered(1, c, zcats[1])
        for d in range(3, 0, -1):
            direct = row >= d
            across = 8 * column + 2 * lax.rem(row - d + 4, 4) + h
            for k in range(2):
                e = 2 * d + 1 - k
                msg[e, cut, :] = first[e - 1] + second[e]
                target = jnp.where(direct, 2 * (p - d) + k, across)
                slot = 2 * d + jnp.where(direct, h, k)
                send = copy(msg.at[e, cut], recv.at[slot, cut], base + P_FWD + e,
                            base + P_FWD + slot, lon(target))
                send.start()
                pending.append(send)
        msg[1, cut, :] = first[0] + second[1]
        msg[0, cut, :] = second[0]
        rel[0, cut, :] = jnp.zeros((RAYS, IMP), F32)
        rel[1, cut, :] = first[7]
        near = copy(msg.at[h, cut], recv.at[h, cut], S_NEAR + c, base + P_FWD + h, lon(sib))
        near.start()
        pending.append(near)
        recv[h, cut, :] = msg[1 - h, cut, :]

    cross, bcross, spread = {}, {}, {}

    def relay(c):
        cut = pl.ds(c * RAYS, RAYS)
        base = S_PART + c * P_N
        for d in range(3, 0, -1):
            @pl.when(row + d > 3)
            def _(d=d):
                for k in range(2):
                    arrived(recv.at[2 * d + k, cut], base + P_FWD + 2 * d + k)
                    rel[k, cut, :] += recv[2 * d + k, cut, :]

        for k in range(2):
            cross[c, k] = copy(rel.at[k, cut], xr.at[h, cut], base + P_FX + k, base + P_FX + h,
                               lon(other + k))
        cross[c, 1].start()
        pending.append(cross[c, 1])

        @pl.when(row > 0)
        def _():
            cross[c, 0].start()

    def own(c):
        cut = pl.ds(c * RAYS, RAYS)
        base = S_PART + c * P_N
        arrived(recv.at[1 - h, cut], base + P_FWD + 1 - h)
        for s in range(2):
            adx[s, cut, :] = recv[s, cut, :]
        for d in range(1, 4):
            @pl.when(row + d <= 3)
            def _(d=d):
                for s in range(2):
                    arrived(recv.at[2 * d + s, cut], base + P_FWD + 2 * d + s)
                    adx[s, cut, :] += recv[2 * d + s, cut, :]

        @pl.when(row + h > 0)
        def _():
            for s in range(2):
                arrived(xr.at[s, cut], base + P_FX + s)
                adx[s, cut, :] += xr[s, cut, :]

        for s in range(2):
            rows = slice(s * HALF + c * RAYS, s * HALF + (c + 1) * RAYS)
            bent = adx[s, cut, :]
            bend_ref[rows, :] = bent
            adx[s, cut, :] = (bent - obs_ref[rows, :]) / (err_ref[rows, :] * err_ref[rows, :])
        for s in range(2):
            bcross[c, s] = copy(adx.at[s, cut], adx.at[2 + h, cut], base + P_BX + s,
                                base + P_BX + h, lon(other + s))

        @pl.when(row + h > 0)
        def _():
            bcross[c, 0].start()
            bcross[c, 1].start()

        for d in range(1, 4):
            direct = row + d <= 3
            below = 8 * column + 2 * lax.rem(row + d, 4)
            for k in range(2):
                e = 2 * d + 1 - jnp.where(direct, h, k)
                spread[c, d, k] = copy(
                    adx.at[jnp.where(direct, k, 2 + k), cut], adjr.at[e, cut],
                    base + P_BWD + 2 * d - 1 + k, base + P_BWD + e,
                    lon(below + jnp.where(direct, k, h)))
                pending.append(spread[c, d, k])
        for d in range(3, 0, -1):
            @pl.when(row + d <= 3)
            def _(d=d):
                spread[c, d, 0].start()
                spread[c, d, 1].start()
        bnear = copy(adx.at[1 - h, cut], adjr.at[1 - h, cut], S_BNEAR + c, base + P_BWD + 1 - h,
                     lon(sib))
        bnear.start()
        pending.append(bnear)
        adjr[1 - h, cut, :] = adx[h, cut, :]

    def pass_on(c):
        cut = pl.ds(c * RAYS, RAYS)
        base = S_PART + c * P_N

        @pl.when(row > 0)
        def _():
            arrived(adx.at[2, cut], base + P_BX)

        arrived(adx.at[3, cut], base + P_BX + 1)
        for d in range(3, 0, -1):
            @pl.when(row + d > 3)
            def _(d=d):
                spread[c, d, 0].start()
                spread[c, d, 1].start()
        adjr[8, cut, :] = adx[3, cut, :]

    def collect(c):
        cut = pl.ds(c * RAYS, RAYS)
        base = S_PART + c * P_N + P_BWD
        arrived(adjr.at[h, cut], base + h)
        for e in range(2, 8):
            arrived(adjr.at[e, cut], base + e)
        for t in range(2):
            for o in range(SPAN):
                k = t * SPAN + o
                hi, lo = split_hi_lo(
                    adjr[o + 1 - t, cut, :] * w_t[c * RAYS : (c + 1) * RAYS, k : k + 1])
                rhs[t, c, o * RAYS : (o + 1) * RAYS, 0:256] = hi
                rhs[t, c, o * RAYS : (o + 1) * RAYS, 256:512] = lo

    def scattered(t, c):
        got = jnp.dot(ohb[t, c], rhs[t, c], preferred_element_type=F32)
        return got[:, :256] + got[:, 256:]

    for c in range(PARTS):
        push(c)
    for t in range(2):
        for c in range(PARTS):
            for q in range(SPAN * RAYS // 128):
                n = 128 // RAYS
                line = jnp.concatenate(
                    [cols_row[t * SPAN + q * n + o : t * SPAN + q * n + o + 1,
                              c * RAYS : (c + 1) * RAYS] for o in range(n)], axis=1)
                ohb[t, c, :, q * 128 : (q + 1) * 128] = jnp.where(
                    row_ids == line, 1.0, 0.0).astype(BF16)
    level_matrix(cw_ref, wb, False)
    t_mix = jnp.concatenate([t_hi[:64], t_lo[:64], t_hi[:64], t_lo[:64]], axis=0)
    for m in range(4):
        for q in range(2):
            keep = lax.rem(iota((256, CH), 0) // NQ, 8) == 2 * m + q
            wr[m * 256 : (m + 1) * 256, q * 128 : (q + 1) * 128] = jnp.where(
                keep, t_mix, 0.0).astype(BF16)
    relay(0)
    own(0)
    for c in range(1, PARTS):
        relay(c)
        pass_on(c - 1)
        own(c)
    pass_on(PARTS - 1)
    for c in range(PARTS):
        collect(c)
        part = scattered(1 - h, c)
        dzs[...] = part if c == 0 else dzs[...] + part
        if c < PARTS - 1:
            part = scattered(h, c)
            dzm[...] = part if c == 0 else dzm[...] + part
    dz_copy = copy(dzs, dzr, S_DZ, S_DZ, lon(sib))
    dz_copy.start()
    pending.append(dz_copy)
    mine_dz = dzm[...] + scattered(h, PARTS - 1)
    arrived(dzr, S_DZ)
    d_hi, d_lo = split_hi_lo(mine_dz + dzr[...])
    contract = (((1,), (1,)), ((), ()))
    dprof = (lax.dot_general(d_hi, kb[:, 0:256], contract, preferred_element_type=F32)
             + lax.dot_general(d_lo, kb[:, 0:256], contract, preferred_element_type=F32)
             + lax.dot_general(d_hi, kb[:, 256:512], contract, preferred_element_type=F32))
    low = iota((COLS, 128), 1) < 64
    for b in range(4):
        part = dprof[:, b * 128 : (b + 1) * 128]
        other = pltpu.roll(part, 64, 1)
        for q in range(2):
            dup = jnp.where(low, part, other) if q == 0 else jnp.where(low, other, part)
            hi, lo = split_hi_lo(dup)
            dpb[2 * b + q, :, 0:128] = hi
            dpb[2 * b + q, :, 128:256] = lo

    def store(b):
        return pltpu.make_async_copy(
            xs.at[pl.ds(8 * b + 1, 8)], gx_out.at[pl.ds(8 * b, 8)], osem.at[b])

    for b in range(8):
        def slopes(m, carry, b=b):
            df = jnp.dot(dpb[b], wr[pl.ds(m * 256, 256), :], preferred_element_type=F32)
            l = 8 * b + 2 * m
            da[l + 1] = (df[:, :128] * dsv[l]).astype(BF16)
            da[l + 2] = (df[:, 128:] * dsv[l + 1]).astype(BF16)
            return carry

        lax.fori_loop(0, 4, slopes, 0, unroll=4)

    acc[...] = jnp.zeros_like(acc)

    def outer(n, carry):
        four, two = [], []
        for m in (2 * n, 2 * n + 1):
            four.append(jnp.concatenate([da[2 * m + d] for d in range(4)], axis=1))
            two.append(jnp.concatenate([xs[2 * m + 1], xs[2 * m + 2]], axis=1))
        acc[...] += lax.dot_general(
            jnp.concatenate(two, axis=0), jnp.concatenate(four, axis=0),
            (((0,), (0,)), ((), ())), preferred_element_type=F32)
        return carry

    lax.fori_loop(0, 16, outer, 0, unroll=2)

    def state_levels(b):
        def pair(n, carry):
            l = 8 * b + 2 * n
            d4 = jnp.concatenate([da[l + d] for d in range(4)], axis=1)
            g = jnp.dot(d4, wb[...], preferred_element_type=F32)
            xs[l + 1] = g[:, :128].astype(BF16)
            xs[l + 2] = g[:, 128:].astype(BF16)
            return carry

        lax.fori_loop(0, 4, pair, 0, unroll=4)
        store(b).start()

    same = iota((CH, CH), 0) // 16 == iota((CH, CH), 1) // 16
    taps = []
    for t in range(3):
        full = (acc[0:128, (2 - t) * 128 : (3 - t) * 128]
                + acc[128:256, (3 - t) * 128 : (4 - t) * 128])
        taps.append(jnp.sum(jnp.where(same, full, 0.0).reshape(8, 16, CH), axis=0))
    flat = jnp.concatenate(taps, axis=0)
    g0[0] = flat[0:24]
    g0[1] = flat[24:48]
    g1[i] = g0[h]
    r1 = [copy(g0.at[lax.rem(i + d, 2)], g1.at[i], S_R1 + d, S_R1 + i, lon(i + d))
          for d in range(1, 16)]
    for c in r1:
        c.start()
    pending.extend(r1)
    for b in range(5):
        state_levels(b)
    for d in range(1, 16):
        k = lax.rem(i + d, 16)
        arrived(g1.at[k], S_R1 + k)
    total = g1[0]
    for k in range(1, 16):
        total = total + g1[k]
    g2[h, j] = total
    r2 = [copy(g2.at[h, j], g2.at[h, j], S_R2, S_R2 + 8 * h + j, {"lon": sib, "lat": j})]
    for d in range(1, 8):
        for n, u in enumerate((i, sib)):
            r2.append(copy(g2.at[h, j], g2.at[h, j], S_R2 + 2 * d - 1 + n, S_R2 + 8 * h + j,
                           {"lon": u, "lat": lax.rem(j + d, 8)}))
    for c in r2:
        c.start()
    pending.extend(r2)
    for b in range(5, 8):
        state_levels(b)
    arrived(g2.at[1 - h, j], S_R2 + 8 * (1 - h) + j)
    for d in range(1, 8):
        k = lax.rem(j + d, 8)
        arrived(g2.at[h, k], S_R2 + 8 * h + k)
        arrived(g2.at[1 - h, k], S_R2 + 8 * (1 - h) + k)
    for s in range(2):
        total = g2[s, 0]
        for k in range(1, 8):
            total = total + g2[s, k]
        gc_ref[24 * s : 24 * (s + 1), :] = total

    for c in pending:
        c.wait_send()

    @pl.when(row > 0)
    def _():
        for c in range(PARTS):
            cross[c, 0].wait_send()

    @pl.when(row + h > 0)
    def _():
        for c in range(PARTS):
            bcross[c, 0].wait_send()
            bcross[c, 1].wait_send()

    for b in range(8):
        store(b).wait()


def on_device(state, conv_w, readout, kernel, cross_col, seg_count, seg_len, observed, obs_err):
    vm = pl.BlockSpec(memory_space=pltpu.VMEM)
    hbm = pl.BlockSpec(memory_space=pl.ANY)
    sds = jax.ShapeDtypeStruct
    v = pltpu.VMEM
    dma = pltpu.SemaphoreType.DMA
    bending, grad_x, grad = pl.pallas_call(
        forward_kernel,
        out_shape=(sds((256, IMP), F32), sds((LEV, COLS, CH), BF16), sds((48, CH), F32)),
        in_specs=[hbm] + [vm] * 8,
        out_specs=(vm, hbm, vm),
        scratch_shapes=[
            v((LEV + 2, COLS, CH), BF16), v((LEV, COLS, CH), F32), v((LEV + 2, COLS, CH), BF16),
            v((512, 256), BF16), v((512, 256), BF16), v((2048, 256), BF16), v((1024, 256), BF16),
            v((512, 512), BF16), v((512, 256), F32), v((512, 512), F32),
            [v((512, 256), F32)] * 4, [v((512, 256), BF16)] * 4, v((10, 1, 256), jnp.int32),
            v((2, 8, 256), jnp.int32), v((2, 8, 256), F32), v((2, COLS, IMP), F32),
            v((2, 1024, 512), BF16), v((2, PARTS, 512, SPAN * RAYS), BF16),
            v((9, HALF, IMP), F32), v((8, HALF, IMP), F32), v((2, HALF, IMP), F32),
            v((2, HALF, IMP), F32), v((4, HALF, IMP), F32), v((9, HALF, IMP), F32),
            v((2, PARTS, SPAN * RAYS, 512), BF16),
            v((COLS, IMP), F32), v((COLS, IMP), F32), v((COLS, IMP), F32),
            v((8, 512, 256), BF16), v((256, 512), F32),
            v((2, 24, CH), F32), v((16, 24, CH), F32), v((2, 8, 24, CH), F32),
            dma((NCHUNK,)), dma((NCHUNK,)), dma((S_N,)), dma((S_N,)),
        ],
        compiler_params=pltpu.CompilerParams(
            vmem_limit_bytes=60 << 20, collective_id=0, has_side_effects=True),
        name="bend",
    )(state[0, 0], conv_w, readout.T, kernel.transpose(1, 2, 0).reshape(LQ, IMP), cross_col[0, 0],
      seg_count[0], seg_len[0, 0], observed[0, 0], obs_err[0, 0])
    grad_conv = grad.reshape(3, 16, 8, 16).transpose(0, 2, 1, 3)
    return grad_x[None, None], bending[None, None], grad_conv


def solution(mesh):
    in_specs = (
        P("lon", "lat", None, None, None),
        P(),
        P(),
        P(),
        P("lon", "lat", None, None),
        P("lon", "lat", None),
        P("lon", "lat", None, None),
        P("lon", "lat", None, None),
        P("lon", "lat", None, None),
    )
    out_specs = (P("lon", "lat", None, None, None), P("lon", "lat", None, None), P())
    return jax.shard_map(
        on_device, mesh=mesh, in_specs=in_specs, out_specs=out_specs, check_vma=False
    )
```

```python
import functools

import jax
import jax.numpy as jnp
from jax import lax
from jax.experimental import pallas as pl
from jax.experimental.pallas import tpu as pltpu
from jax.sharding import PartitionSpec as P

F32 = jnp.float32
BF16 = jnp.bfloat16
LEV, COLS, CH, NQ, IMP, LQ = 64, 512, 128, 8, 256, 512
SPAN, HALF = 8, 128
CHUNK = 8
NCHUNK = LEV // CHUNK
MESH = pl.DeviceIdType.MESH

PARTS = 2
RAYS = HALF // PARTS
S_CNT, S_CC, S_SL, S_DZ, S_NEAR, S_BNEAR, S_R1, S_R2, S_PART = 0, 10, 11, 12, 13, 17, 21, 37, 53
P_Z, P_FWD, P_FX, P_BX, P_BWD, P_N = 0, 1, 9, 11, 13, 22
S_N = S_PART + PARTS * P_N


def split_hi_lo(value):
    hi = value.astype(BF16)
    return hi, (value - hi.astype(F32)).astype(BF16)


def iota(shape, dim):
    return lax.broadcasted_iota(jnp.int32, shape, dim)


def wide_tap(cw_ref, tap):
    flat = cw_ref[tap].astype(F32).reshape(CH, 16).astype(BF16)
    pick = jnp.where(iota((16, CH), 0) == lax.rem(iota((16, CH), 1), 16), 1.0, 0.0).astype(BF16)
    full = jnp.dot(flat, pick, preferred_element_type=F32)
    return jnp.where(iota((CH, CH), 0) // 16 == iota((CH, CH), 1) // 16, full, 0.0)


def level_matrix(cw_ref, out_ref, forward):
    taps = [wide_tap(cw_ref, t) for t in range(3)]
    for d in range(4):
        for p in range(2):
            t = d - p if forward else p + 2 - d
            if 0 <= t <= 2:
                block = taps[t] if forward else taps[t].T
            else:
                block = jnp.zeros((CH, CH), F32)
            out_ref[d * CH : (d + 1) * CH, p * CH : (p + 1) * CH] = block.astype(BF16)


def forward_kernel(
    state_ref, cw_ref, rt_ref, kt_hbm, cc_ref, sc_ref, sl_ref, obs_hbm, err_hbm,
    bend_ref, gx_out, gc_ref,
    xs, dsv, da, wf, wb, wm, wr, kb, pacc, prof, acts, feats, cnt, cca, sla, zabs, ohf, ohb,
    msg, recv, rel, xr, adx, adjr, dzr, acc, g0, g1, g2, kt_ref, obs_ref, err_ref, xt,
    isem, osem, ssem, rsem,
):
    i = lax.axis_index("lon")
    j = lax.axis_index("lat")
    h = lax.rem(i, 2)
    p = i // 2
    row = lax.rem(p, 4)
    column = p // 4
    sib = i + 1 - 2 * h

    def lon(u):
        return {"lon": lax.rem(u + 32, 16)}

    def copy(src, dst, s, r, dev):
        return pltpu.make_async_remote_copy(
            src_ref=src, dst_ref=dst, send_sem=ssem.at[s], recv_sem=rsem.at[r],
            device_id=dev, device_id_type=MESH)

    def arrived(dst, r):
        copy(dst, dst, r, r, lon(sib)).wait_recv()

    def load(c):
        return pltpu.make_async_copy(
            state_ref.at[pl.ds(c * CHUNK, CHUNK)], xs.at[pl.ds(1 + c * CHUNK, CHUNK)], isem.at[c])

    late = [pltpu.make_async_copy(src, dst, isem.at[NCHUNK + n]) for n, (src, dst) in enumerate(
        ((kt_hbm, kt_ref), (obs_hbm, obs_ref), (err_hbm, err_ref)))]
    for c in range(NCHUNK):
        load(c).start()
    for c in late:
        c.start()
    barrier = pltpu.get_barrier_semaphore()
    for d in range(1, 16):
        pl.semaphore_signal(barrier, inc=1, device_id=lon(i + d), device_id_type=MESH)
    for d in range(1, 8):
        for u in (i, sib):
            pl.semaphore_signal(barrier, inc=1, device_id={"lon": u, "lat": lax.rem(j + d, 8)},
                                device_id_type=MESH)

    zero = jnp.zeros((COLS, CH), BF16)
    xs[0] = zero
    xs[LEV + 1] = zero
    da[0] = zero
    da[LEV + 1] = zero
    level_matrix(cw_ref, wf, True)
    tiled = jnp.concatenate([rt_ref[...]] * 16, axis=0)
    t_hi, t_lo = split_hi_lo(tiled)
    t_hi, t_lo = t_hi.astype(F32), t_lo.astype(F32)
    for m in range(8):
        for q in range(2):
            keep = iota((CH, CH), 1) // NQ == 2 * m + q
            rows = slice(m * 256 + q * 128, m * 256 + q * 128 + 128)
            wm[rows, 0:128] = jnp.where(keep, t_hi.T, 0.0).astype(BF16)
            wm[rows, 128:256] = jnp.where(keep, t_lo.T, 0.0).astype(BF16)
    def convolve(m):
        x4 = jnp.concatenate([xs[2 * m + d] for d in range(4)], axis=1)
        return jnp.dot(x4, wf[...], preferred_element_type=F32)

    def activate(k, m):
        act = acts[k][...]
        sig = 0.5 * jnp.tanh(0.5 * act) + 0.5
        feat = act * sig
        slope = sig + feat * (1.0 - sig)
        dsv[2 * m] = slope[:, :128]
        dsv[2 * m + 1] = slope[:, 128:]
        feats[k][...] = feat.astype(BF16)

    def read_out(a, k):
        both = jnp.concatenate([feats[a][...], feats[a + 1][...]], axis=1)
        pacc[...] += jnp.dot(both, wm[pl.ds(k * 256, 512), :], preferred_element_type=F32)

    early = [copy(sc_ref, cnt.at[1 - h], S_CNT, S_CNT + 1 - h, lon(sib)),
             copy(cc_ref, cca.at[h], S_CC, S_CC, lon(sib)),
             copy(sl_ref, sla.at[h], S_SL, S_SL, lon(sib))]
    for d in range(1, 5):
        for k in range(2):
            early.append(copy(sc_ref, cnt.at[2 * d + 1 - h], S_CNT + 2 * d - 1 + k,
                              S_CNT + 2 * d + 1 - h, lon(2 * (p + d) + k)))
    pending = list(early)
    cnt[1 - h] = sc_ref[...]
    cca[h] = cc_ref[...]
    sla[h] = sl_ref[...]

    load(0).wait()
    acts[0][...] = convolve(0)
    acts[1][...] = convolve(1)
    for b in range(4):
        pacc[...] = jnp.zeros_like(pacc)
        for half in range(2):
            if (b, half) == (2, 0):
                pl.semaphore_wait(barrier, 29)
                for c in early:
                    c.start()
            ahead = 2 * b + half + 1
            if ahead < NCHUNK:
                load(ahead).wait()
            m = b * 8 + half * 4
            acts[2][...] = convolve(m + 2)
            activate(0, m)
            acts[3][...] = convolve(m + 3)
            activate(1, m + 1)
            read_out(0, 4 * half)
            if m + 4 < 32:
                acts[0][...] = convolve(m + 4)
            activate(2, m + 2)
            if m + 5 < 32:
                acts[1][...] = convolve(m + 5)
            activate(3, m + 3)
            read_out(2, 4 * half + 2)
        prof[:, b % 2 * 128 : b % 2 * 128 + 128] = pacc[:, :128] + pacc[:, 128:]
        if b == 0:
            late[0].wait()
            kb_hi, kb_lo = split_hi_lo(kt_ref[...])
            kb[:, 0:256] = kb_hi
            kb[:, 256:512] = kb_lo
        if b % 2 == 1:
            rows = slice((b - 1) * 128, (b + 1) * 128)
            p_hi, p_lo = split_hi_lo(prof[...])
            zz = jnp.dot(p_hi, kb[rows, :], preferred_element_type=F32)
            zz = (zz[:, :256] + zz[:, 256:]
                  + jnp.dot(p_lo, kb[rows, 0:256], preferred_element_type=F32))
            if b == 1:
                zabs[h] = zz
            else:
                zabs[h] += zz

    z_copy = copy(zabs.at[h], zabs.at[h], S_PART + P_Z, S_PART + P_Z, lon(sib))
    z_copy.start()
    pending.append(z_copy)

    arrived(cca.at[1 - h], S_CC)
    arrived(sla.at[1 - h], S_SL)
    arrived(cnt.at[h], S_CNT + h)
    for e in range(2, 10):
        arrived(cnt.at[e], S_CNT + e)

    def mine(row):
        return jnp.where(h == 0, row[:, :HALF], row[:, HALF:])

    cols_row = jnp.concatenate(
        [mine(cca[0]), mine(cca[1]), jnp.zeros((112, HALF), jnp.int32)], axis=0)
    weights = []
    for t in range(2):
        lens = mine(sla[t])
        for o in range(SPAN):
            count = mine(cnt[o + 1 - t])
            weights.append(lens[o : o + 1] * jnp.where(count > o, 1.0, 0.0))
    w_row = jnp.concatenate(weights + [jnp.zeros((112, HALF), F32)], axis=0)
    cols_t = cols_row.astype(F32).T.astype(jnp.int32)
    w_t = w_row.T
    lane_ids = iota((HALF, COLS), 1)
    row_ids = iota((COLS, HALF), 0)
    for t in range(2):
        for o in range(SPAN):
            k = t * SPAN + o
            for c in range(PARTS):
                ohf[t, (c * SPAN + o) * RAYS : (c * SPAN + o + 1) * RAYS, :] = jnp.where(
                    lane_ids[:RAYS] == cols_t[c * RAYS : (c + 1) * RAYS, k : k + 1], 1.0, 0.0
                ).astype(BF16)

    def gathered(t, c, zcat):
        got = jnp.dot(ohf[t, c * SPAN * RAYS : (c + 1) * SPAN * RAYS, :], zcat,
                      preferred_element_type=F32)
        got = got[:, :256] + got[:, 256:]
        return [got[o * RAYS : (o + 1) * RAYS]
                * w_t[c * RAYS : (c + 1) * RAYS, t * SPAN + o : t * SPAN + o + 1]
                for o in range(SPAN)]

    arrived(zabs.at[1 - h], S_PART + P_Z)
    zcats = [jnp.concatenate(split_hi_lo(zabs[t]), axis=1) for t in range(2)]
    other = 8 * (1 - column) + 2 * row

    def push(c):
        cut = pl.ds(c * RAYS, RAYS)
        base = S_PART + c * P_N
        first, second = gathered(0, c, zcats[0]), gathered(1, c, zcats[1])
        for d in range(3, 0, -1):
            direct = row >= d
            across = 8 * column + 2 * lax.rem(row - d + 4, 4) + h
            for k in range(2):
                e = 2 * d + 1 - k
                msg[e, cut, :] = first[e - 1] + second[e]
                target = jnp.where(direct, 2 * (p - d) + k, across)
                slot = 2 * d + jnp.where(direct, h, k)
                send = copy(msg.at[e, cut], recv.at[slot, cut], base + P_FWD + e,
                            base + P_FWD + slot, lon(target))
                send.start()
                pending.append(send)
        msg[1, cut, :] = first[0] + second[1]
        msg[0, cut, :] = second[0]
        rel[0, cut, :] = jnp.zeros((RAYS, IMP), F32)
        rel[1, cut, :] = first[7]
        near = copy(msg.at[h, cut], recv.at[h, cut], S_NEAR + c, base + P_FWD + h, lon(sib))
        near.start()
        pending.append(near)
        recv[h, cut, :] = msg[1 - h, cut, :]

    cross, bcross, spread = {}, {}, {}

    def relay(c):
        cut = pl.ds(c * RAYS, RAYS)
        base = S_PART + c * P_N
        for d in range(3, 0, -1):
            @pl.when(row + d > 3)
            def _(d=d):
                for k in range(2):
                    arrived(recv.at[2 * d + k, cut], base + P_FWD + 2 * d + k)
                    rel[k, cut, :] += recv[2 * d + k, cut, :]

        for k in range(2):
            cross[c, k] = copy(rel.at[k, cut], xr.at[h, cut], base + P_FX + k, base + P_FX + h,
                               lon(other + k))
        cross[c, 1].start()
        pending.append(cross[c, 1])

        @pl.when(row > 0)
        def _():
            cross[c, 0].start()

    def own(c):
        cut = pl.ds(c * RAYS, RAYS)
        base = S_PART + c * P_N
        arrived(recv.at[1 - h, cut], base + P_FWD + 1 - h)
        for s in range(2):
            adx[s, cut, :] = recv[s, cut, :]
        for d in range(1, 4):
            @pl.when(row + d <= 3)
            def _(d=d):
                for s in range(2):
                    arrived(recv.at[2 * d + s, cut], base + P_FWD + 2 * d + s)
                    adx[s, cut, :] += recv[2 * d + s, cut, :]

        @pl.when(row + h > 0)
        def _():
            for s in range(2):
                arrived(xr.at[s, cut], base + P_FX + s)
                adx[s, cut, :] += xr[s, cut, :]

        for s in range(2):
            rows = slice(s * HALF + c * RAYS, s * HALF + (c + 1) * RAYS)
            bent = adx[s, cut, :]
            bend_ref[rows, :] = bent
            adx[s, cut, :] = (bent - obs_ref[rows, :]) / (err_ref[rows, :] * err_ref[rows, :])
        for s in range(2):
            bcross[c, s] = copy(adx.at[s, cut], adx.at[2 + h, cut], base + P_BX + s,
                                base + P_BX + h, lon(other + s))

        @pl.when(row + h > 0)
        def _():
            bcross[c, 0].start()
            bcross[c, 1].start()

        for d in range(1, 4):
            direct = row + d <= 3
            below = 8 * column + 2 * lax.rem(row + d, 4)
            for k in range(2):
                e = 2 * d + 1 - jnp.where(direct, h, k)
                spread[c, d, k] = copy(
                    adx.at[jnp.where(direct, k, 2 + k), cut], adjr.at[e, cut],
                    base + P_BWD + 2 * d - 1 + k, base + P_BWD + e,
                    lon(below + jnp.where(direct, k, h)))
                pending.append(spread[c, d, k])
        for d in range(3, 0, -1):
            @pl.when(row + d <= 3)
            def _(d=d):
                spread[c, d, 0].start()
                spread[c, d, 1].start()
        bnear = copy(adx.at[1 - h, cut], adjr.at[1 - h, cut], S_BNEAR + c, base + P_BWD + 1 - h,
                     lon(sib))
        bnear.start()
        pending.append(bnear)
        adjr[1 - h, cut, :] = adx[h, cut, :]

    def pass_on(c):
        cut = pl.ds(c * RAYS, RAYS)
        base = S_PART + c * P_N

        @pl.when(row > 0)
        def _():
            arrived(adx.at[2, cut], base + P_BX)

        arrived(adx.at[3, cut], base + P_BX + 1)
        for d in range(3, 0, -1):
            @pl.when(row + d > 3)
            def _(d=d):
                spread[c, d, 0].start()
                spread[c, d, 1].start()
        adjr[8, cut, :] = adx[3, cut, :]

    def collect(c):
        cut = pl.ds(c * RAYS, RAYS)
        base = S_PART + c * P_N + P_BWD
        arrived(adjr.at[h, cut], base + h)
        for e in range(2, 8):
            arrived(adjr.at[e, cut], base + e)
        for t in range(2):
            for o in range(SPAN):
                k = t * SPAN + o
                hi, lo = split_hi_lo(
                    adjr[o + 1 - t, cut, :] * w_t[c * RAYS : (c + 1) * RAYS, k : k + 1])
                ohf[t, (c * SPAN + o) * RAYS : (c * SPAN + o + 1) * RAYS, 0:256] = hi
                ohf[t, (c * SPAN + o) * RAYS : (c * SPAN + o + 1) * RAYS, 256:512] = lo

    def scattered(t, c):
        got = jnp.dot(ohb[t, c], ohf[t, c * SPAN * RAYS : (c + 1) * SPAN * RAYS, :], preferred_element_type=F32)
        return got[:, :256] + got[:, 256:]

    for c in range(PARTS):
        push(c)
    for t in range(2):
        for c in range(PARTS):
            for q in range(SPAN * RAYS // 128):
                n = 128 // RAYS
                line = jnp.concatenate(
                    [cols_row[t * SPAN + q * n + o : t * SPAN + q * n + o + 1,
                              c * RAYS : (c + 1) * RAYS] for o in range(n)], axis=1)
                ohb[t, c, :, q * 128 : (q + 1) * 128] = jnp.where(
                    row_ids == line, 1.0, 0.0).astype(BF16)
    level_matrix(cw_ref, wb, False)

    def turn(n, carry):
        xt[n, 0:128, :] = xs[2 * n + 1].T
        xt[n, 128:256, :] = xs[2 * n + 2].T
        return carry

    lax.fori_loop(0, 32, turn, 0, unroll=2)
    t_mix = jnp.concatenate([t_hi[:64], t_lo[:64], t_hi[:64], t_lo[:64]], axis=0)
    for m in range(4):
        for q in range(2):
            keep = lax.rem(iota((256, CH), 0) // NQ, 8) == 2 * m + q
            wr[m * 256 : (m + 1) * 256, q * 128 : (q + 1) * 128] = jnp.where(
                keep, t_mix, 0.0).astype(BF16)
    relay(0)
    late[1].wait()
    late[2].wait()
    own(0)
    for c in range(1, PARTS):
        relay(c)
        pass_on(c - 1)
        own(c)
    pass_on(PARTS - 1)
    dzs, dzm = acts[0], acts[1]
    for c in range(PARTS):
        collect(c)
        part = scattered(1 - h, c)
        dzs[...] = part if c == 0 else dzs[...] + part
        if c < PARTS - 1:
            part = scattered(h, c)
            dzm[...] = part if c == 0 else dzm[...] + part
    dz_copy = copy(dzs, dzr, S_DZ, S_DZ, lon(sib))
    dz_copy.start()
    pending.append(dz_copy)
    mine_dz = dzm[...] + scattered(h, PARTS - 1)
    arrived(dzr, S_DZ)
    d_hi, d_lo = split_hi_lo(mine_dz + dzr[...])
    contract = (((1,), (1,)), ((), ()))
    dprof = (lax.dot_general(d_hi, kb[:, 0:256], contract, preferred_element_type=F32)
             + lax.dot_general(d_lo, kb[:, 0:256], contract, preferred_element_type=F32)
             + lax.dot_general(d_hi, kb[:, 256:512], contract, preferred_element_type=F32))
    low = iota((COLS, 128), 1) < 64
    for b in range(4):
        part = dprof[:, b * 128 : (b + 1) * 128]
        other = pltpu.roll(part, 64, 1)
        for q in range(2):
            dup = jnp.where(low, part, other) if q == 0 else jnp.where(low, other, part)
            hi, lo = split_hi_lo(dup)
            ohb[b // 2, b % 2, :, q * 256 : q * 256 + 128] = hi
            ohb[b // 2, b % 2, :, q * 256 + 128 : q * 256 + 256] = lo

    def store(b):
        return pltpu.make_async_copy(
            xs.at[pl.ds(8 * b + 1, 8)], gx_out.at[pl.ds(8 * b, 8)], osem.at[b])

    for b in range(8):
        def slopes(m, carry, b=b):
            df = jnp.dot(ohb[b // 4, b // 2 % 2, :, b % 2 * 256 : b % 2 * 256 + 256], wr[pl.ds(m * 256, 256), :], preferred_element_type=F32)
            l = 8 * b + 2 * m
            da[l + 1] = (df[:, :128] * dsv[l]).astype(BF16)
            da[l + 2] = (df[:, 128:] * dsv[l + 1]).astype(BF16)
            return carry

        lax.fori_loop(0, 4, slopes, 0, unroll=4)

    acc[...] = jnp.zeros_like(acc)

    def outer(n, carry):
        four, two = [], []
        for m in (2 * n, 2 * n + 1):
            four.append(jnp.concatenate([da[2 * m + d] for d in range(4)], axis=1))
            two.append(xt[m])
        acc[...] += lax.dot_general(
            jnp.concatenate(two, axis=1), jnp.concatenate(four, axis=0),
            (((1,), (0,)), ((), ())), preferred_element_type=F32)
        return carry

    lax.fori_loop(0, 16, outer, 0, unroll=2)

    def state_levels(b):
        def pair(n, carry):
            l = 8 * b + 2 * n
            d4 = jnp.concatenate([da[l + d] for d in range(4)], axis=1)
            g = jnp.dot(d4, wb[...], preferred_element_type=F32)
            xs[l + 1] = g[:, :128].astype(BF16)
            xs[l + 2] = g[:, 128:].astype(BF16)
            return carry

        lax.fori_loop(0, 4, pair, 0, unroll=4)
        store(b).start()

    same = iota((CH, CH), 0) // 16 == iota((CH, CH), 1) // 16
    taps = []
    for t in range(3):
        full = (acc[0:128, (2 - t) * 128 : (3 - t) * 128]
                + acc[128:256, (3 - t) * 128 : (4 - t) * 128])
        taps.append(jnp.sum(jnp.where(same, full, 0.0).reshape(8, 16, CH), axis=0))
    flat = jnp.concatenate(taps, axis=0)
    g0[0] = flat[0:24]
    g0[1] = flat[24:48]
    g1[i] = g0[h]
    r1 = [copy(g0.at[lax.rem(i + d, 2)], g1.at[i], S_R1 + d, S_R1 + i, lon(i + d))
          for d in range(1, 16)]
    for c in r1:
        c.start()
    pending.extend(r1)
    for b in range(5):
        state_levels(b)
    for d in range(1, 16):
        k = lax.rem(i + d, 16)
        arrived(g1.at[k], S_R1 + k)
    total = g1[0]
    for k in range(1, 16):
        total = total + g1[k]
    g2[h, j] = total
    r2 = [copy(g2.at[h, j], g2.at[h, j], S_R2, S_R2 + 8 * h + j, {"lon": sib, "lat": j})]
    for d in range(1, 8):
        for n, u in enumerate((i, sib)):
            r2.append(copy(g2.at[h, j], g2.at[h, j], S_R2 + 2 * d - 1 + n, S_R2 + 8 * h + j,
                           {"lon": u, "lat": lax.rem(j + d, 8)}))
    for c in r2:
        c.start()
    pending.extend(r2)
    for b in range(5, 8):
        state_levels(b)
    arrived(g2.at[1 - h, j], S_R2 + 8 * (1 - h) + j)
    for d in range(1, 8):
        k = lax.rem(j + d, 8)
        arrived(g2.at[h, k], S_R2 + 8 * h + k)
        arrived(g2.at[1 - h, k], S_R2 + 8 * (1 - h) + k)
    for s in range(2):
        total = g2[s, 0]
        for k in range(1, 8):
            total = total + g2[s, k]
        for n in range(3):
            t, r = (24 * s + 8 * n) // 16, (24 * s + 8 * n) % 16
            for g in range(8):
                gc_ref[t, g, r : r + 8, :] = total[8 * n : 8 * n + 8, 16 * g : 16 * g + 16]

    for c in pending:
        c.wait_send()

    @pl.when(row > 0)
    def _():
        for c in range(PARTS):
            cross[c, 0].wait_send()

    @pl.when(row + h > 0)
    def _():
        for c in range(PARTS):
            bcross[c, 0].wait_send()
            bcross[c, 1].wait_send()

    for b in range(8):
        store(b).wait()


def on_device(state, conv_w, readout, kernel, cross_col, seg_count, seg_len, observed, obs_err):
    vm = pl.BlockSpec(memory_space=pltpu.VMEM)
    hbm = pl.BlockSpec(memory_space=pl.ANY)
    sds = jax.ShapeDtypeStruct
    v = pltpu.VMEM
    dma = pltpu.SemaphoreType.DMA
    bending, grad_x, grad = pl.pallas_call(
        forward_kernel,
        out_shape=(sds((256, IMP), F32), sds((LEV, COLS, CH), BF16), sds((3, 8, 16, 16), F32)),
        in_specs=[hbm, vm, vm, hbm, vm, vm, vm, hbm, hbm],
        out_specs=(vm, hbm, vm),
        scratch_shapes=[
            v((LEV + 2, COLS, CH), BF16), v((LEV, COLS, CH), F32), v((LEV + 2, COLS, CH), BF16),
            v((512, 256), BF16), v((512, 256), BF16), v((2048, 256), BF16), v((1024, 256), BF16),
            v((512, 512), BF16), v((512, 256), F32), v((512, 256), F32),
            [v((512, 256), F32)] * 4, [v((512, 256), BF16)] * 4, v((10, 1, 256), jnp.int32),
            v((2, 8, 256), jnp.int32), v((2, 8, 256), F32), v((2, COLS, IMP), F32),
            v((2, 1024, 512), BF16), v((2, PARTS, 512, SPAN * RAYS), BF16),
            v((9, HALF, IMP), F32), v((8, HALF, IMP), F32), v((2, HALF, IMP), F32),
            v((2, HALF, IMP), F32), v((4, HALF, IMP), F32), v((9, HALF, IMP), F32),
            v((COLS, IMP), F32),
            v((256, 512), F32),
            v((2, 24, CH), F32), v((16, 24, CH), F32), v((2, 8, 24, CH), F32),
            v((LQ, IMP), F32), v((256, IMP), F32), v((256, IMP), F32),
            v((32, 256, 512), BF16),
            dma((NCHUNK + 3,)), dma((NCHUNK,)), dma((S_N,)), dma((S_N,)),
        ],
        compiler_params=pltpu.CompilerParams(
            vmem_limit_bytes=61 << 20, collective_id=0, has_side_effects=True),
        name="bend",
    )(state[0, 0], conv_w, readout.T, kernel.transpose(1, 2, 0).reshape(LQ, IMP), cross_col[0, 0],
      seg_count[0], seg_len[0, 0], observed[0, 0], obs_err[0, 0])
    return grad_x[None, None], bending[None, None], grad


def solution(mesh):
    in_specs = (
        P("lon", "lat", None, None, None),
        P(),
        P(),
        P(),
        P("lon", "lat", None, None),
        P("lon", "lat", None),
        P("lon", "lat", None, None),
        P("lon", "lat", None, None),
        P("lon", "lat", None, None),
    )
    out_specs = (P("lon", "lat", None, None, None), P("lon", "lat", None, None), P())
    return jax.shard_map(
        on_device, mesh=mesh, in_specs=in_specs, out_specs=out_specs, check_vma=False
    )
```

```python
import functools

import jax
import jax.numpy as jnp
from jax import lax
from jax.experimental import pallas as pl
from jax.experimental.pallas import tpu as pltpu
from jax.sharding import PartitionSpec as P

F32 = jnp.float32
BF16 = jnp.bfloat16
LEV, COLS, CH, NQ, IMP, LQ = 64, 512, 128, 8, 256, 512
SPAN, HALF = 8, 128
CHUNK = 8
NCHUNK = LEV // CHUNK
MESH = pl.DeviceIdType.MESH

PARTS = 2
RAYS = HALF // PARTS
S_CNT, S_CC, S_SL, S_DZ, S_NEAR, S_BNEAR, S_R1, S_R2, S_PART = 0, 10, 11, 12, 13, 17, 21, 37, 53
P_Z, P_FWD, P_FX, P_BX, P_BWD, P_N = 0, 1, 9, 11, 13, 22
S_N = S_PART + PARTS * P_N


def split_hi_lo(value):
    hi = value.astype(BF16)
    return hi, (value - hi.astype(F32)).astype(BF16)


def iota(shape, dim):
    return lax.broadcasted_iota(jnp.int32, shape, dim)


def wide_tap(cw_ref, tap):
    flat = cw_ref[tap].astype(F32).reshape(CH, 16).astype(BF16)
    pick = jnp.where(iota((16, CH), 0) == lax.rem(iota((16, CH), 1), 16), 1.0, 0.0).astype(BF16)
    full = jnp.dot(flat, pick, preferred_element_type=F32)
    return jnp.where(iota((CH, CH), 0) // 16 == iota((CH, CH), 1) // 16, full, 0.0)


def level_matrix(cw_ref, out_ref, forward):
    taps = [wide_tap(cw_ref, t) for t in range(3)]
    for d in range(4):
        for p in range(2):
            t = d - p if forward else p + 2 - d
            if 0 <= t <= 2:
                block = taps[t] if forward else taps[t].T
            else:
                block = jnp.zeros((CH, CH), F32)
            out_ref[d * CH : (d + 1) * CH, p * CH : (p + 1) * CH] = block.astype(BF16)


def forward_kernel(
    state_ref, cw_ref, rt_ref, kt_hbm, cc_ref, sc_ref, sl_ref, obs_hbm, err_hbm,
    bend_ref, gx_out, gc_ref,
    xs, dsv, da, wf, wb, wm, wr, kb, pacc, prof, acts, feats, cnt, cca, sla, zabs, ohf, ohb,
    msg, recv, rel, xr, adx, adjr, dzr, acc, g0, g1, g2, kt_ref, obs_ref, err_ref, xt,
    isem, osem, ssem, rsem,
):
    i = lax.axis_index("lon")
    j = lax.axis_index("lat")
    h = lax.rem(i, 2)
    p = i // 2
    row = lax.rem(p, 4)
    column = p // 4
    sib = i + 1 - 2 * h

    def lon(u):
        return {"lon": lax.rem(u + 32, 16)}

    def copy(src, dst, s, r, dev):
        return pltpu.make_async_remote_copy(
            src_ref=src, dst_ref=dst, send_sem=ssem.at[s], recv_sem=rsem.at[r],
            device_id=dev, device_id_type=MESH)

    def arrived(dst, r):
        copy(dst, dst, r, r, lon(sib)).wait_recv()

    def load(c):
        return pltpu.make_async_copy(
            state_ref.at[pl.ds(c * CHUNK, CHUNK)], xs.at[pl.ds(1 + c * CHUNK, CHUNK)], isem.at[c])

    late = [pltpu.make_async_copy(src, dst, isem.at[NCHUNK + n]) for n, (src, dst) in enumerate(
        ((kt_hbm, kt_ref), (obs_hbm, obs_ref), (err_hbm, err_ref)))]
    for c in range(NCHUNK):
        load(c).start()
    for c in late:
        c.start()
    barrier = pltpu.get_barrier_semaphore()
    for d in range(1, 16):
        pl.semaphore_signal(barrier, inc=1, device_id=lon(i + d), device_id_type=MESH)
    for d in range(1, 8):
        for u in (i, sib):
            pl.semaphore_signal(barrier, inc=1, device_id={"lon": u, "lat": lax.rem(j + d, 8)},
                                device_id_type=MESH)

    zero = jnp.zeros((COLS, CH), BF16)
    xs[0] = zero
    xs[LEV + 1] = zero
    da[0] = zero
    da[LEV + 1] = zero
    level_matrix(cw_ref, wf, True)
    tiled = jnp.concatenate([rt_ref[...]] * 16, axis=0)
    t_hi, t_lo = split_hi_lo(tiled)
    t_hi, t_lo = t_hi.astype(F32), t_lo.astype(F32)
    for m in range(8):
        for q in range(2):
            keep = iota((CH, CH), 1) // NQ == 2 * m + q
            rows = slice(m * 256 + q * 128, m * 256 + q * 128 + 128)
            wm[rows, 0:128] = jnp.where(keep, t_hi.T, 0.0).astype(BF16)
            wm[rows, 128:256] = jnp.where(keep, t_lo.T, 0.0).astype(BF16)
    def convolve(m):
        x4 = jnp.concatenate([xs[2 * m + d] for d in range(4)], axis=1)
        return jnp.dot(x4, wf[...], preferred_element_type=F32)

    def activate(k, m):
        act = acts[k][...]
        sig = 0.5 * jnp.tanh(0.5 * act) + 0.5
        feat = act * sig
        slope = sig + feat * (1.0 - sig)
        dsv[2 * m] = slope[:, :128]
        dsv[2 * m + 1] = slope[:, 128:]
        feats[k][...] = feat.astype(BF16)

    def read_out(a, k):
        both = jnp.concatenate([feats[a][...], feats[a + 1][...]], axis=1)
        pacc[...] += jnp.dot(both, wm[pl.ds(k * 256, 512), :], preferred_element_type=F32)

    early = [copy(sc_ref, cnt.at[1 - h], S_CNT, S_CNT + 1 - h, lon(sib)),
             copy(cc_ref, cca.at[h], S_CC, S_CC, lon(sib)),
             copy(sl_ref, sla.at[h], S_SL, S_SL, lon(sib))]
    for d in range(1, 5):
        for k in range(2):
            early.append(copy(sc_ref, cnt.at[2 * d + 1 - h], S_CNT + 2 * d - 1 + k,
                              S_CNT + 2 * d + 1 - h, lon(2 * (p + d) + k)))
    pending = list(early)
    cnt[1 - h] = sc_ref[...]
    cca[h] = cc_ref[...]
    sla[h] = sl_ref[...]

    load(0).wait()
    acts[0][...] = convolve(0)
    acts[1][...] = convolve(1)
    for b in range(4):
        pacc[...] = jnp.zeros_like(pacc)
        for half in range(2):
            if (b, half) == (2, 0):
                pl.semaphore_wait(barrier, 29)
                for c in early:
                    c.start()
            ahead = 2 * b + half + 1
            if ahead < NCHUNK:
                load(ahead).wait()
            m = b * 8 + half * 4
            acts[2][...] = convolve(m + 2)
            activate(0, m)
            acts[3][...] = convolve(m + 3)
            activate(1, m + 1)
            read_out(0, 4 * half)
            if m + 4 < 32:
                acts[0][...] = convolve(m + 4)
            activate(2, m + 2)
            if m + 5 < 32:
                acts[1][...] = convolve(m + 5)
            activate(3, m + 3)
            read_out(2, 4 * half + 2)
        prof[:, b % 2 * 128 : b % 2 * 128 + 128] = pacc[:, :128] + pacc[:, 128:]
        if b == 0:
            late[0].wait()
            kb_hi, kb_lo = split_hi_lo(kt_ref[...])
            kb[:, 0:256] = kb_hi
            kb[:, 256:512] = kb_lo
        if b % 2 == 1:
            rows = slice((b - 1) * 128, (b + 1) * 128)
            p_hi, p_lo = split_hi_lo(prof[...])
            zz = jnp.dot(p_hi, kb[rows, :], preferred_element_type=F32)
            zz = (zz[:, :256] + zz[:, 256:]
                  + jnp.dot(p_lo, kb[rows, 0:256], preferred_element_type=F32))
            if b == 1:
                zabs[h] = zz
            else:
                zabs[h] += zz

    z_copy = copy(zabs.at[h], zabs.at[h], S_PART + P_Z, S_PART + P_Z, lon(sib))
    z_copy.start()
    pending.append(z_copy)

    arrived(cca.at[1 - h], S_CC)
    arrived(sla.at[1 - h], S_SL)
    arrived(cnt.at[h], S_CNT + h)
    for e in range(2, 10):
        arrived(cnt.at[e], S_CNT + e)

    def mine(row):
        return jnp.where(h == 0, row[:, :HALF], row[:, HALF:])

    cols_row = jnp.concatenate(
        [mine(cca[0]), mine(cca[1]), jnp.zeros((112, HALF), jnp.int32)], axis=0)
    weights = []
    for t in range(2):
        lens = mine(sla[t])
        for o in range(SPAN):
            count = mine(cnt[o + 1 - t])
            weights.append(lens[o : o + 1] * jnp.where(count > o, 1.0, 0.0))
    w_row = jnp.concatenate(weights + [jnp.zeros((112, HALF), F32)], axis=0)
    cols_t = cols_row.astype(F32).T.astype(jnp.int32)
    w_t = w_row.T
    lane_ids = iota((HALF, COLS), 1)
    row_ids = iota((COLS, HALF), 0)
    for t in range(2):
        for o in range(SPAN):
            k = t * SPAN + o
            for c in range(PARTS):
                ohf[t, (c * SPAN + o) * RAYS : (c * SPAN + o + 1) * RAYS, :] = jnp.where(
                    lane_ids[:RAYS] == cols_t[c * RAYS : (c + 1) * RAYS, k : k + 1], 1.0, 0.0
                ).astype(BF16)

    def gathered(t, c, zcat):
        got = jnp.dot(ohf[t, c * SPAN * RAYS : (c + 1) * SPAN * RAYS, :], zcat,
                      preferred_element_type=F32)
        got = got[:, :256] + got[:, 256:]
        return [got[o * RAYS : (o + 1) * RAYS]
                * w_t[c * RAYS : (c + 1) * RAYS, t * SPAN + o : t * SPAN + o + 1]
                for o in range(SPAN)]

    arrived(zabs.at[1 - h], S_PART + P_Z)
    zcats = [jnp.concatenate(split_hi_lo(zabs[t]), axis=1) for t in range(2)]
    other = 8 * (1 - column) + 2 * row

    def push(c):
        cut = pl.ds(c * RAYS, RAYS)
        base = S_PART + c * P_N
        first, second = gathered(0, c, zcats[0]), gathered(1, c, zcats[1])
        for d in range(3, 0, -1):
            direct = row >= d
            across = 8 * column + 2 * lax.rem(row - d + 4, 4) + h
            for k in range(2):
                e = 2 * d + 1 - k
                msg[e, cut, :] = first[e - 1] + second[e]
                target = jnp.where(direct, 2 * (p - d) + k, across)
                slot = 2 * d + jnp.where(direct, h, k)
                send = copy(msg.at[e, cut], recv.at[slot, cut], base + P_FWD + e,
                            base + P_FWD + slot, lon(target))
                send.start()
                pending.append(send)
        msg[1, cut, :] = first[0] + second[1]
        msg[0, cut, :] = second[0]
        rel[0, cut, :] = jnp.zeros((RAYS, IMP), F32)
        rel[1, cut, :] = first[7]
        near = copy(msg.at[h, cut], recv.at[h, cut], S_NEAR + c, base + P_FWD + h, lon(sib))
        near.start()
        pending.append(near)
        recv[h, cut, :] = msg[1 - h, cut, :]

    cross, bcross, spread = {}, {}, {}

    def relay(c):
        cut = pl.ds(c * RAYS, RAYS)
        base = S_PART + c * P_N
        for d in range(3, 0, -1):
            @pl.when(row + d > 3)
            def _(d=d):
                for k in range(2):
                    arrived(recv.at[2 * d + k, cut], base + P_FWD + 2 * d + k)
                    rel[k, cut, :] += recv[2 * d + k, cut, :]

        for k in range(2):
            cross[c, k] = copy(rel.at[k, cut], xr.at[h, cut], base + P_FX + k, base + P_FX + h,
                               lon(other + k))
        cross[c, 1].start()
        pending.append(cross[c, 1])

        @pl.when(row > 0)
        def _():
            cross[c, 0].start()

    def own(c):
        cut = pl.ds(c * RAYS, RAYS)
        base = S_PART + c * P_N
        arrived(recv.at[1 - h, cut], base + P_FWD + 1 - h)
        for s in range(2):
            adx[s, cut, :] = recv[s, cut, :]
        for d in range(1, 4):
            @pl.when(row + d <= 3)
            def _(d=d):
                for s in range(2):
                    arrived(recv.at[2 * d + s, cut], base + P_FWD + 2 * d + s)
                    adx[s, cut, :] += recv[2 * d + s, cut, :]

        @pl.when(row + h > 0)
        def _():
            for s in range(2):
                arrived(xr.at[s, cut], base + P_FX + s)
                adx[s, cut, :] += xr[s, cut, :]

        for s in range(2):
            rows = slice(s * HALF + c * RAYS, s * HALF + (c + 1) * RAYS)
            bent = adx[s, cut, :]
            bend_ref[rows, :] = bent
            adx[s, cut, :] = (bent - obs_ref[rows, :]) / (err_ref[rows, :] * err_ref[rows, :])
        for s in range(2):
            bcross[c, s] = copy(adx.at[s, cut], adx.at[2 + h, cut], base + P_BX + s,
                                base + P_BX + h, lon(other + s))

        @pl.when(row + h > 0)
        def _():
            bcross[c, 0].start()
            bcross[c, 1].start()

        for d in range(1, 4):
            direct = row + d <= 3
            below = 8 * column + 2 * lax.rem(row + d, 4)
            for k in range(2):
                e = 2 * d + 1 - jnp.where(direct, h, k)
                spread[c, d, k] = copy(
                    adx.at[jnp.where(direct, k, 2 + k), cut], adjr.at[e, cut],
                    base + P_BWD + 2 * d - 1 + k, base + P_BWD + e,
                    lon(below + jnp.where(direct, k, h)))
                pending.append(spread[c, d, k])
        for d in range(3, 0, -1):
            @pl.when(row + d <= 3)
            def _(d=d):
                spread[c, d, 0].start()
                spread[c, d, 1].start()
        bnear = copy(adx.at[1 - h, cut], adjr.at[1 - h, cut], S_BNEAR + c, base + P_BWD + 1 - h,
                     lon(sib))
        bnear.start()
        pending.append(bnear)
        adjr[1 - h, cut, :] = adx[h, cut, :]

    def pass_on(c):
        cut = pl.ds(c * RAYS, RAYS)
        base = S_PART + c * P_N

        @pl.when(row > 0)
        def _():
            arrived(adx.at[2, cut], base + P_BX)

        arrived(adx.at[3, cut], base + P_BX + 1)
        for d in range(3, 0, -1):
            @pl.when(row + d > 3)
            def _(d=d):
                spread[c, d, 0].start()
                spread[c, d, 1].start()
        adjr[8, cut, :] = adx[3, cut, :]

    def collect(c):
        cut = pl.ds(c * RAYS, RAYS)
        base = S_PART + c * P_N + P_BWD
        arrived(adjr.at[h, cut], base + h)
        for e in range(2, 8):
            arrived(adjr.at[e, cut], base + e)
        for t in range(2):
            for o in range(SPAN):
                k = t * SPAN + o
                hi, lo = split_hi_lo(
                    adjr[o + 1 - t, cut, :] * w_t[c * RAYS : (c + 1) * RAYS, k : k + 1])
                ohf[t, (c * SPAN + o) * RAYS : (c * SPAN + o + 1) * RAYS, 0:256] = hi
                ohf[t, (c * SPAN + o) * RAYS : (c * SPAN + o + 1) * RAYS, 256:512] = lo

    def scattered(t, c):
        got = jnp.dot(ohb[t, c], ohf[t, c * SPAN * RAYS : (c + 1) * SPAN * RAYS, :], preferred_element_type=F32)
        return got[:, :256] + got[:, 256:]

    for c in range(PARTS):
        push(c)
    for t in range(2):
        for c in range(PARTS):
            for q in range(SPAN * RAYS // 128):
                n = 128 // RAYS
                line = jnp.concatenate(
                    [cols_row[t * SPAN + q * n + o : t * SPAN + q * n + o + 1,
                              c * RAYS : (c + 1) * RAYS] for o in range(n)], axis=1)
                ohb[t, c, :, q * 128 : (q + 1) * 128] = jnp.where(
                    row_ids == line, 1.0, 0.0).astype(BF16)
    level_matrix(cw_ref, wb, False)

    def turn(n, carry):
        xt[n, 0:128, :] = xs[2 * n + 1].T
        xt[n, 128:256, :] = xs[2 * n + 2].T
        return carry

    lax.fori_loop(0, 32, turn, 0, unroll=4)
    t_mix = jnp.concatenate([t_hi[:64], t_lo[:64], t_hi[:64], t_lo[:64]], axis=0)
    for m in range(4):
        for q in range(2):
            keep = lax.rem(iota((256, CH), 0) // NQ, 8) == 2 * m + q
            wr[m * 256 : (m + 1) * 256, q * 128 : (q + 1) * 128] = jnp.where(
                keep, t_mix, 0.0).astype(BF16)
    relay(0)
    late[1].wait()
    late[2].wait()
    own(0)
    for c in range(1, PARTS):
        relay(c)
        pass_on(c - 1)
        own(c)
    pass_on(PARTS - 1)
    dzs, dzm = acts[0], acts[1]
    for c in range(PARTS):
        collect(c)
        part = scattered(1 - h, c)
        dzs[...] = part if c == 0 else dzs[...] + part
        if c < PARTS - 1:
            part = scattered(h, c)
            dzm[...] = part if c == 0 else dzm[...] + part
    dz_copy = copy(dzs, dzr, S_DZ, S_DZ, lon(sib))
    dz_copy.start()
    pending.append(dz_copy)
    mine_dz = dzm[...] + scattered(h, PARTS - 1)
    arrived(dzr, S_DZ)
    d_hi, d_lo = split_hi_lo(mine_dz + dzr[...])
    contract = (((1,), (1,)), ((), ()))
    dprof = (lax.dot_general(d_hi, kb[:, 0:256], contract, preferred_element_type=F32)
             + lax.dot_general(d_lo, kb[:, 0:256], contract, preferred_element_type=F32)
             + lax.dot_general(d_hi, kb[:, 256:512], contract, preferred_element_type=F32))
    low = iota((COLS, 128), 1) < 64
    for b in range(4):
        part = dprof[:, b * 128 : (b + 1) * 128]
        other = pltpu.roll(part, 64, 1)
        for q in range(2):
            dup = jnp.where(low, part, other) if q == 0 else jnp.where(low, other, part)
            hi, lo = split_hi_lo(dup)
            ohb[b // 2, b % 2, :, q * 256 : q * 256 + 128] = hi
            ohb[b // 2, b % 2, :, q * 256 + 128 : q * 256 + 256] = lo

    def store(b):
        return pltpu.make_async_copy(
            xs.at[pl.ds(8 * b + 1, 8)], gx_out.at[pl.ds(8 * b, 8)], osem.at[b])

    for b in range(8):
        def slopes(m, carry, b=b):
            df = jnp.dot(ohb[b // 4, b // 2 % 2, :, b % 2 * 256 : b % 2 * 256 + 256], wr[pl.ds(m * 256, 256), :], preferred_element_type=F32)
            l = 8 * b + 2 * m
            da[l + 1] = (df[:, :128] * dsv[l]).astype(BF16)
            da[l + 2] = (df[:, 128:] * dsv[l + 1]).astype(BF16)
            return carry

        lax.fori_loop(0, 4, slopes, 0, unroll=4)

    acc[...] = jnp.zeros_like(acc)

    def outer(n, carry):
        four, two = [], []
        for m in (2 * n, 2 * n + 1):
            four.append(jnp.concatenate([da[2 * m + d] for d in range(4)], axis=1))
            two.append(xt[m])
        acc[...] += lax.dot_general(
            jnp.concatenate(two, axis=1), jnp.concatenate(four, axis=0),
            (((1,), (0,)), ((), ())), preferred_element_type=F32)
        return carry

    lax.fori_loop(0, 16, outer, 0, unroll=4)

    def state_levels(b):
        def pair(n, carry):
            l = 8 * b + 2 * n
            d4 = jnp.concatenate([da[l + d] for d in range(4)], axis=1)
            g = jnp.dot(d4, wb[...], preferred_element_type=F32)
            xs[l + 1] = g[:, :128].astype(BF16)
            xs[l + 2] = g[:, 128:].astype(BF16)
            return carry

        lax.fori_loop(0, 4, pair, 0, unroll=4)
        store(b).start()

    same = iota((CH, CH), 0) // 16 == iota((CH, CH), 1) // 16
    taps = []
    for t in range(3):
        full = (acc[0:128, (2 - t) * 128 : (3 - t) * 128]
                + acc[128:256, (3 - t) * 128 : (4 - t) * 128])
        taps.append(jnp.sum(jnp.where(same, full, 0.0).reshape(8, 16, CH), axis=0))
    flat = jnp.concatenate(taps, axis=0)
    g0[0] = flat[0:24]
    g0[1] = flat[24:48]
    g1[i] = g0[h]
    r1 = [copy(g0.at[lax.rem(i + d, 2)], g1.at[i], S_R1 + d, S_R1 + i, lon(i + d))
          for d in range(1, 16)]
    for c in r1:
        c.start()
    pending.extend(r1)
    for b in range(5):
        state_levels(b)
    for d in range(1, 16):
        k = lax.rem(i + d, 16)
        arrived(g1.at[k], S_R1 + k)
    total = g1[0]
    for k in range(1, 16):
        total = total + g1[k]
    g2[h, j] = total
    r2 = [copy(g2.at[h, j], g2.at[h, j], S_R2, S_R2 + 8 * h + j, {"lon": sib, "lat": j})]
    for d in range(1, 8):
        for n, u in enumerate((i, sib)):
            r2.append(copy(g2.at[h, j], g2.at[h, j], S_R2 + 2 * d - 1 + n, S_R2 + 8 * h + j,
                           {"lon": u, "lat": lax.rem(j + d, 8)}))
    for c in r2:
        c.start()
    pending.extend(r2)
    for b in range(5, 8):
        state_levels(b)
    arrived(g2.at[1 - h, j], S_R2 + 8 * (1 - h) + j)
    for d in range(1, 8):
        k = lax.rem(j + d, 8)
        arrived(g2.at[h, k], S_R2 + 8 * h + k)
        arrived(g2.at[1 - h, k], S_R2 + 8 * (1 - h) + k)
    for s in range(2):
        total = g2[s, 0]
        for k in range(1, 8):
            total = total + g2[s, k]
        for n in range(3):
            t, r = (24 * s + 8 * n) // 16, (24 * s + 8 * n) % 16
            for g in range(8):
                gc_ref[t, g, r : r + 8, :] = total[8 * n : 8 * n + 8, 16 * g : 16 * g + 16]

    for c in pending:
        c.wait_send()

    @pl.when(row > 0)
    def _():
        for c in range(PARTS):
            cross[c, 0].wait_send()

    @pl.when(row + h > 0)
    def _():
        for c in range(PARTS):
            bcross[c, 0].wait_send()
            bcross[c, 1].wait_send()

    for b in range(8):
        store(b).wait()


def on_device(state, conv_w, readout, kernel, cross_col, seg_count, seg_len, observed, obs_err):
    vm = pl.BlockSpec(memory_space=pltpu.VMEM)
    hbm = pl.BlockSpec(memory_space=pl.ANY)
    sds = jax.ShapeDtypeStruct
    v = pltpu.VMEM
    dma = pltpu.SemaphoreType.DMA
    bending, grad_x, grad = pl.pallas_call(
        forward_kernel,
        out_shape=(sds((256, IMP), F32), sds((LEV, COLS, CH), BF16), sds((3, 8, 16, 16), F32)),
        in_specs=[hbm, vm, vm, hbm, vm, vm, vm, hbm, hbm],
        out_specs=(vm, hbm, vm),
        scratch_shapes=[
            v((LEV + 2, COLS, CH), BF16), v((LEV, COLS, CH), F32), v((LEV + 2, COLS, CH), BF16),
            v((512, 256), BF16), v((512, 256), BF16), v((2048, 256), BF16), v((1024, 256), BF16),
            v((512, 512), BF16), v((512, 256), F32), v((512, 256), F32),
            [v((512, 256), F32)] * 4, [v((512, 256), BF16)] * 4, v((10, 1, 256), jnp.int32),
            v((2, 8, 256), jnp.int32), v((2, 8, 256), F32), v((2, COLS, IMP), F32),
            v((2, 1024, 512), BF16), v((2, PARTS, 512, SPAN * RAYS), BF16),
            v((9, HALF, IMP), F32), v((8, HALF, IMP), F32), v((2, HALF, IMP), F32),
            v((2, HALF, IMP), F32), v((4, HALF, IMP), F32), v((9, HALF, IMP), F32),
            v((COLS, IMP), F32),
            v((256, 512), F32),
            v((2, 24, CH), F32), v((16, 24, CH), F32), v((2, 8, 24, CH), F32),
            v((LQ, IMP), F32), v((256, IMP), F32), v((256, IMP), F32),
            v((32, 256, 512), BF16),
            dma((NCHUNK + 3,)), dma((NCHUNK,)), dma((S_N,)), dma((S_N,)),
        ],
        compiler_params=pltpu.CompilerParams(
            vmem_limit_bytes=61 << 20, collective_id=0, has_side_effects=True),
        name="bend",
    )(state[0, 0], conv_w, readout.T, kernel.transpose(1, 2, 0).reshape(LQ, IMP), cross_col[0, 0],
      seg_count[0], seg_len[0, 0], observed[0, 0], obs_err[0, 0])
    return grad_x[None, None], bending[None, None], grad


def solution(mesh):
    in_specs = (
        P("lon", "lat", None, None, None),
        P(),
        P(),
        P(),
        P("lon", "lat", None, None),
        P("lon", "lat", None),
        P("lon", "lat", None, None),
        P("lon", "lat", None, None),
        P("lon", "lat", None, None),
    )
    out_specs = (P("lon", "lat", None, None, None), P("lon", "lat", None, None), P())
    return jax.shard_map(
        on_device, mesh=mesh, in_specs=in_specs, out_specs=out_specs, check_vma=False
    )
```
